256 devices in a mesh: fsdp: 16 (over z_hi, y, core), gossip: 16 (over z_lo, x).
Axes of the slice: x: 4, y: 4, z: 8 (z_hi: 2, z_lo: 4; z = z_hi * 4 + z_lo), core: 2. Of those that a mesh axis runs over, the one named last changes fastest.
Arguments:
- tokens: bfloat16 [2, 16, 2048, 5120], P(None, 'gossip', 'fsdp'), may hold values from -0.14941406 to 0.14941406
- master: float32 [16, 5120, 256], P('gossip', 'fsdp'), may hold values from -0.3 to 0.3
- moment: float32 [16, 5120, 256], P('gossip', 'fsdp'), may hold values from -4 to 4
- second: float32 [16, 5120, 256], P('gossip', 'fsdp'), may hold values from 0.1 to 2
- cube_bit: int32 [4], replicated, may hold values from 0 to 2
Outputs:
- averaged: float32 [16, 5120, 256], P('gossip', 'fsdp')
- moment_out: float32 [16, 5120, 256], P('gossip', 'fsdp')
- second_out: float32 [16, 5120, 256], P('gossip', 'fsdp')
The draws below stay inside these ranges and needn't reach their ends.
Inputs may be any that keep to these rules, and one draw needn't show every extreme that they name: In round r replica g pairs with replica g xor 2^cube_bit[r].
All inputs are finite; a program needn't handle non-finite values.
Results may differ from the reference program's by a relative error of at most 0.006.
Values may be sent and summed in bfloat16 or wider, within the bound.
A program may use at most 64 MiB of HBM per device.

```python
import jax
import jax.numpy as jnp
from jax import lax

D = 5120
RANK = 128
STEPS = 2
ROUNDS = 4
TOK_DEV = 128
GROUP_TOK = 2048
REPLICAS = 16


def set_ends(result, stream_key, least, largest):
    dims = result.shape
    spot = [jax.random.randint(jax.random.fold_in(stream_key, axis), (), 0, dims[axis]) for axis in range(len(dims))]
    result = result.at[tuple(spot)].set(least)
    longest = dims.index(max(dims))
    spot[longest] = (spot[longest] + 1) % dims[longest]
    return result.at[tuple(spot)].set(largest)


def shard_levels(rng, dims, cuts, least, largest):
    level = 1.0
    for dim, parts in cuts:
        draws = jax.random.uniform(jax.random.fold_in(jax.random.fold_in(rng, 6), dim), (parts,), jnp.float32, least / len(cuts), largest / len(cuts))
        level = level * jnp.repeat(jnp.exp(draws), dims[dim] // parts).reshape((-1,) + (1,) * (len(dims) - 1 - dim))
    return level


def bell_draw(own_key, extent, width, bound, cuts=(), kind=jnp.bfloat16):
    entries = jax.random.normal(own_key, extent, jnp.float32) * width
    if len(cuts) > 0:
        entries = shard_levels(own_key, extent, cuts, -0.22, 0.18) * entries
    return jnp.clip(entries, min=-bound, max=bound).astype(kind)


def setup_inputs(seed: int = 0) -> dict:
    arg_keys = jax.random.split(jax.random.key(seed), 6)
    return {
        "tokens": bell_draw(arg_keys[0], (STEPS, REPLICAS, GROUP_TOK, D), 0.025, 0.14941406, ((1, 16), (2, 16))),
        "master": bell_draw(arg_keys[1], (REPLICAS, D, 2 * RANK), 0.05, 0.3, ((0, 16), (1, 16)), jnp.float32),
        "moment": bell_draw(arg_keys[2], (REPLICAS, D, 2 * RANK), 0.5, 4.0, ((0, 16), (1, 16)), jnp.float32),
        "second": jnp.clip(0.1 + 1.9 * jax.random.uniform(arg_keys[3], (REPLICAS, D, 2 * RANK), jnp.float32) ** shard_levels(arg_keys[3], (REPLICAS, D, 2 * RANK), ((0, 16), (1, 16)), -0.2, 0.2), 0.1, 2.0),
        "cube_bit": set_ends(jax.random.randint(arg_keys[4], (ROUNDS,), 0, 3), jax.random.fold_in(arg_keys[4], 1), 0, 2).astype(jnp.int32),
    }


def train_steps(packed):
    params, first, squares, rows_all = packed
    for section in range(STEPS):
        weights = params.astype(jnp.bfloat16)
        left_part = weights[:, :RANK]
        right_part = weights[:, RANK:]
        xfloat = rows_all[section].astype(jnp.float32)
        scaled = xfloat * lax.rsqrt(lax.optimization_barrier(jnp.mean(xfloat * xfloat, axis=-1, keepdims=True)) + 1e-05)
        normed = scaled.astype(jnp.bfloat16)
        low = (jnp.dot(normed, left_part, preferred_element_type=jnp.float32) * D ** (-0.5)).astype(jnp.bfloat16)
        out = xfloat + RANK ** (-0.5) * jnp.dot(low, right_part.T, preferred_element_type=jnp.float32)
        inverse = lax.rsqrt(lax.optimization_barrier(jnp.mean(out * out, axis=-1, keepdims=True)) + 1e-05)
        zvalue = out * inverse
        following = jnp.concatenate([scaled[1:], jnp.zeros((1, D), jnp.float32)], axis=0)
        position = jnp.arange(GROUP_TOK, dtype=jnp.int32)
        keeping = ((position + 1) % TOK_DEV != 0).astype(jnp.float32)[:, None]
        dzvalue = (RANK / GROUP_TOK) ** 0.5 * (zvalue - following) * keeping
        d_out = (inverse * (dzvalue - zvalue * lax.optimization_barrier(jnp.mean(dzvalue * zvalue, axis=-1, keepdims=True)))).astype(jnp.bfloat16)
        grad_right = jnp.dot(d_out.T, low, preferred_element_type=jnp.float32) * RANK ** (-0.5)
        d_low = (jnp.dot(d_out, right_part, preferred_element_type=jnp.float32) * (RANK * D) ** (-0.5)).astype(jnp.bfloat16)
        grad_left = jnp.dot(normed.T, d_low, preferred_element_type=jnp.float32)
        grad = jnp.concatenate([grad_left, grad_right], axis=1)
        first = 0.9 * first + 0.1 * grad
        squares = 0.95 * squares + 0.05 * grad * grad
        params = params - 0.02 * first / (jnp.sqrt(squares) + 1e-08)
    return (params, first, squares)

def reference(tokens, master, moment, second, cube_bit):
    params, first, squares = lax.map(train_steps, (master, moment, second, jnp.swapaxes(tokens, 0, 1)))
    replica_ids = jnp.arange(REPLICAS, dtype=jnp.int32)
    for round_index in range(ROUNDS):
        partner = jnp.bitwise_xor(replica_ids, jnp.left_shift(jnp.int32(1), cube_bit[round_index].astype(jnp.int32)))
        params = 0.5 * (params + params[partner])
    return (params, first, squares)
```

```python
import jax
import jax.numpy as jnp
from jax import lax
from jax.experimental import pallas as pl
from jax.experimental.pallas import tpu as pltpu
from jax.sharding import PartitionSpec as P

MESH = pl.DeviceIdType.MESH
F32, BF16 = jnp.float32, jnp.bfloat16

D = 5120
RANK = 128
STEPS = 2
DOC = 128
GROUP_TOK = 2048
ROWS = 320
CHIP_ROWS = 640
HALF = 2560
YS = 4
CHUNKS = 2
CHUNK = ROWS // CHUNKS
GROUP = 8
PART = 48


def part_start(member):
    return pl.multiple_of(16 * ((5 * member) // 2), 16)


def kernel(
    tokens, master, moment, second, cube, avg_out, mom_out, sec_out,
    weight, first, squares, wire_w, docs, xs, xt, xgram, pacc, psend, prec, eall,
    keep_cross, keep_own, dsend, drec, zsend, zrec, grec, gsend, arec,
    send_sem, recv_sem, local_sem,
):
    f = lax.axis_index("fsdp")
    g = lax.axis_index("gossip")
    z, y, c = f // 8, (f // 2) % YS, f % 2
    q = g % GROUP

    def at(fi, gi):
        return {"fsdp": fi, "gossip": gi}

    def y_peer(k):
        return (y + k) % YS

    def y_dev(k):
        return at(z * 8 + y_peer(k) * 2 + c, g)

    core_dev = at(z * 8 + y * 2 + (1 - c), g)
    z_dev = at((1 - z) * 8 + y * 2 + c, g)

    def member(delta):
        bits = [(q // (1 << b)) % 2 for b in range(3)]
        return sum((1 - bits[b] if (delta >> b) & 1 else bits[b]) * (1 << b) for b in range(3))

    def gossip_dev(delta):
        return at(f, g - q + member(delta))

    barrier = pltpu.get_barrier_semaphore()
    peers = [y_dev(k) for k in (1, 2, 3)] + [core_dev, z_dev] + [gossip_dev(d) for d in range(1, GROUP)]
    for peer in peers:
        pl.semaphore_signal(barrier, inc=1, device_id=peer, device_id_type=MESH)

    count = [0, 0]
    sent = []

    def remote(src, dst, device):
        i = count[0]
        count[0] += 1
        copy = pltpu.make_async_remote_copy(
            src_ref=src, dst_ref=dst, send_sem=send_sem.at[i], recv_sem=recv_sem.at[i],
            device_id=device, device_id_type=MESH,
        )
        copy.start()
        sent.append(copy)
        return copy

    def local(src, dst):
        i = count[1]
        count[1] += 1
        copy = pltpu.make_async_copy(src, dst, local_sem.at[i])
        copy.start()
        return copy

    def token_block(s, p, who):
        return tokens.at[s, 0, :, pl.ds(pl.multiple_of(p * HALF + who * CHIP_ROWS, 128), CHIP_ROWS)]

    def doc_rows(who):
        return pl.ds(pl.multiple_of(who * DOC, DOC), DOC)

    in_weight = local(master.at[0], weight)
    in_doc = [local(tokens.at[s, 0], docs.at[s]) for s in range(STEPS)]
    in_own = [[local(token_block(s, p, y), xs.at[s, p, doc_rows(y), :]) for p in (0, 1)] for s in range(STEPS)]
    in_first = local(moment.at[0], first)
    in_squares = local(second.at[0], squares)

    def send_tokens(s):
        return {
            k: [remote(token_block(s, p, y_peer(k)), xs.at[s, p, doc_rows(y), :], y_dev(k)) for p in (0, 1)]
            for k in (1, 3, 2)
        }

    def rows_of(core, chunk=0, size=ROWS):
        return pl.ds(pl.multiple_of(core * ROWS + chunk * CHUNK, 32), size)

    def send_weights(s, chunk):
        own = wire_w.at[s, z, rows_of(c, chunk, CHUNK), :]
        return remote(own, own, z_dev), remote(own, own, core_dev)

    def forward_weights(s, chunk):
        got = wire_w.at[s, 1 - z, rows_of(c, chunk, CHUNK), :]
        return remote(got, got, core_dev)

    in_weight.wait()
    wire_w[0, z, rows_of(c), :] = weight[...].astype(BF16)
    pl.semaphore_wait(barrier, len(peers))

    tok_copies = [None] * STEPS
    w_copies = [send_weights(0, chunk) for chunk in range(CHUNKS)]
    tok_copies[0] = send_tokens(0)

    m = D**-0.5
    r = RANK**-0.5
    alpha = (RANK / GROUP_TOK) ** 0.5
    tall = (DOC, RANK)

    def gram_of(s):
        in_doc[s].wait()
        x = docs[s]
        xgram[s] = lax.dot_general(x, x, (((1,), (1,)), ((), ())), preferred_element_type=F32)

    gram_of(0)

    for s in range(STEPS):
        for chunk in range(CHUNKS):
            w_copies[chunk][1].wait_recv()
        forwards = []
        for chunk in range(CHUNKS):
            w_copies[chunk][0].wait_recv()
            forwards.append(forward_weights(s, chunk))
        for copy in in_own[s]:
            copy.wait()
        for copy in forwards:
            copy.wait_recv()
        gram = jnp.zeros((RANK, RANK), F32)
        for p in (0, 1):
            right = wire_w[s, p, :, RANK:]
            gram += lax.dot_general(right, right, (((0,), (0,)), ((), ())), preferred_element_type=F32)
        gram_wire = gram.astype(BF16)

        def product(who):
            return sum(
                jnp.dot(xs[s, p, doc_rows(who), :], wire_w[s, p], preferred_element_type=F32) for p in (0, 1)
            )

        p_copies = []
        for k in (1, 3, 2):
            for copy in tok_copies[s][YS - k]:
                copy.wait_recv()
            psend[s, k - 1, :, : 2 * RANK] = product(y_peer(k)).astype(BF16)
            psend[s, k - 1, :, 2 * RANK :] = gram_wire
            p_copies.append(remote(psend.at[s, k - 1], prec.at[s, k - 1], y_dev(k)))
        prod = product(y)

        for p in (0, 1):
            xt[p] = xs[s, p].T

        at_t = lax.broadcasted_iota(jnp.int32, tall, 0)
        at_j = lax.broadcasted_iota(jnp.int32, tall, 1)
        xx = xgram[s]
        sx = jnp.sum(jnp.where(at_j == at_t, xx, 0.0), axis=1, keepdims=True)
        xn = jnp.sum(jnp.where(at_j == at_t + 1, xx, 0.0), axis=1, keepdims=True)
        ix = lax.rsqrt(sx * (1.0 / D) + 1e-5)
        ixn = pltpu.roll(jnp.broadcast_to(ix, tall), DOC - 1, 0)[:, :1]
        kept = jnp.where(lax.broadcasted_iota(jnp.int32, (DOC, 1), 0) == DOC - 1, 0.0, alpha)

        for copy in p_copies:
            copy.wait_recv()
        for k in range(3):
            prod += prec[s, k, :, : 2 * RANK].astype(F32)
            gram += prec[s, k, :, 2 * RANK :].astype(F32)

        pl_, pr = prod[:, :RANK], prod[:, RANK:]
        prn = pltpu.roll(pr, DOC - 1, 0)
        low = (ix * pl_ * m).astype(BF16)
        lowf = low.astype(F32)
        ghi = gram.astype(BF16)
        glo = (gram - ghi.astype(F32)).astype(BF16)
        lowg = jnp.dot(low, ghi, preferred_element_type=F32) + jnp.dot(low, glo, preferred_element_type=F32)
        oo = (
            sx
            + (2 * r) * jnp.sum(lowf * pr, axis=1, keepdims=True)
            + (r * r) * jnp.sum(lowf * lowg, axis=1, keepdims=True)
        )
        inv = lax.rsqrt(oo * (1.0 / D) + 1e-5)
        sno = ixn * (xn + r * jnp.sum(lowf * prn, axis=1, keepdims=True))
        cc = kept * (inv * inv * oo - inv * sno) * (1.0 / D)
        aa = inv * inv * (kept - cc)
        bb = kept * inv * ixn
        al = aa * lowf
        dlow = (aa * (pr + r * lowg) - bb * prn) * (RANK * D) ** -0.5
        eall[s, y, :, :RANK] = (ix * dlow).astype(BF16)
        eall[s, y, :, RANK : 2 * RANK] = (r * (al - pltpu.roll(bb * lowf, 1, 0))).astype(BF16)
        eall[s, y, :, 2 * RANK :] = (
            (r * r)
            * lax.dot_general(low, al.astype(BF16), (((0,), (0,)), ((), ())), preferred_element_type=F32)
        ).astype(BF16)
        e_copies = [remote(eall.at[s, y], eall.at[s, y], y_dev(k)) for k in (1, 3, 2)]
        for copy in e_copies:
            copy.wait_recv()
        if s + 1 < STEPS:
            tok_copies[s + 1] = send_tokens(s + 1)

        factor = jnp.concatenate([eall[s, j, :, : 2 * RANK] for j in range(YS)], axis=0)
        outer = sum(eall[s, j, :, 2 * RANK :].astype(F32) for j in range(YS)).astype(BF16)

        def gradient(p, core):
            rows = jnp.dot(xt[p, rows_of(core), :], factor, preferred_element_type=F32)
            more = jnp.dot(wire_w[s, p, rows_of(core), RANK:], outer, preferred_element_type=F32)
            return jnp.concatenate([rows[:, :RANK], rows[:, RANK:] + more], axis=1)

        dsend[s, 0] = gradient(1 - z, 1 - c).astype(BF16)
        cross = remote(dsend.at[s, 0], drec.at[s, 0], core_dev)
        keep_cross[...] = gradient(1 - z, c)
        cross.wait_recv()
        z_copies = []
        for chunk in range(CHUNKS):
            part = pl.ds(chunk * CHUNK, CHUNK)
            zsend[s, part, :] = (keep_cross[part, :] + drec[s, 0, part, :].astype(F32)).astype(BF16)
            z_copies.append(remote(zsend.at[s, part, :], zrec.at[s, part, :], z_dev))
        dsend[s, 1] = gradient(z, 1 - c).astype(BF16)
        own = remote(dsend.at[s, 1], drec.at[s, 1], core_dev)
        keep_own[...] = gradient(z, c)
        own.wait_recv()
        keep_own[...] += drec[s, 1].astype(F32)

        if s == 0:
            in_first.wait()
            in_squares.wait()
            gram_of(1)
        w_copies = []
        for chunk in range(CHUNKS):
            part = pl.ds(chunk * CHUNK, CHUNK)
            z_copies[chunk].wait_recv()
            grad = keep_own[part, :] + zrec[s, part, :].astype(F32)
            one = 0.9 * first[part, :] + 0.1 * grad
            two = 0.95 * squares[part, :] + 0.05 * grad * grad
            new = weight[part, :] - 0.02 * one / (jnp.sqrt(two) + 1e-8)
            first[part, :] = one
            squares[part, :] = two
            weight[part, :] = new
            wire_w[s + 1, z, rows_of(c, chunk, CHUNK), :] = new.astype(BF16)
            if s + 1 < STEPS:
                w_copies.append(send_weights(s + 1, chunk))

    out_first = local(first, mom_out.at[0])
    out_squares = local(squares, sec_out.at[0])

    g_copies = []
    for delta in range(1, GROUP):
        start = c * ROWS + part_start(member(delta))
        rows = pl.ds(pl.multiple_of(start, 16), PART)
        g_copies.append(remote(wire_w.at[STEPS, z, rows, :], grec.at[delta - 1], gossip_dev(delta)))
    share = []
    for b in range(3):
        used = sum((cube[i] == b).astype(jnp.int32) for i in range(4))
        share.append(0.5 * jnp.minimum(used, 1).astype(F32))
    held = [weight[pl.ds(part_start(q), PART), :]]
    for delta in range(1, GROUP):
        g_copies[delta - 1].wait_recv()
        held.append(grec[delta - 1].astype(F32))
    for b in range(3):
        held = [held[d] + share[b] * (held[d ^ (1 << b)] - held[d]) for d in range(GROUP)]
    a_copies = []
    for delta in range(1, GROUP):
        gsend[delta - 1] = held[delta].astype(BF16)
        a_copies.append(remote(gsend.at[delta - 1], arec.at[delta - 1], gossip_dev(delta)))
    avg_out[0, pl.ds(part_start(q), PART), :] = held[0]
    for delta in range(1, GROUP):
        a_copies[delta - 1].wait_recv()
        avg_out[0, pl.ds(part_start(member(delta)), PART), :] = arec[delta - 1].astype(F32)

    for copy in sent:
        copy.wait_send()
    out_first.wait()
    out_squares.wait()


def body(tokens, master, moment, second, cube_bit):
    any_space = pl.BlockSpec(memory_space=pl.ANY)
    vmem = pl.BlockSpec(memory_space=pltpu.VMEM)
    rows = jax.ShapeDtypeStruct((1, ROWS, 2 * RANK), F32)
    wide = 3 * RANK
    n_remote = 3 * STEPS * CHUNKS + STEPS * (6 + 3 + 3 + 2 + CHUNKS) + 2 * (GROUP - 1)
    scratch = [
        pltpu.VMEM((ROWS, 2 * RANK), F32),
        pltpu.VMEM((ROWS, 2 * RANK), F32),
        pltpu.VMEM((ROWS, 2 * RANK), F32),
        pltpu.VMEM((STEPS + 1, 2, CHIP_ROWS, 2 * RANK), BF16),
        pltpu.VMEM((STEPS, DOC, D), BF16),
        pltpu.VMEM((STEPS, 2, YS * DOC, CHIP_ROWS), BF16),
        pltpu.VMEM((2, CHIP_ROWS, YS * DOC), BF16),
        pltpu.VMEM((STEPS, DOC, DOC), F32),
        pltpu.VMEM((DOC, 2 * RANK), F32),
        pltpu.VMEM((STEPS, 3, DOC, wide), BF16),
        pltpu.VMEM((STEPS, 3, DOC, wide), BF16),
        pltpu.VMEM((STEPS, YS, DOC, wide), BF16),
        pltpu.VMEM((ROWS, 2 * RANK), F32),
        pltpu.VMEM((ROWS, 2 * RANK), F32),
        pltpu.VMEM((STEPS, 2, ROWS, 2 * RANK), BF16),
        pltpu.VMEM((STEPS, 2, ROWS, 2 * RANK), BF16),
        pltpu.VMEM((STEPS, ROWS, 2 * RANK), BF16),
        pltpu.VMEM((STEPS, ROWS, 2 * RANK), BF16),
        pltpu.VMEM((GROUP - 1, PART, 2 * RANK), BF16),
        pltpu.VMEM((GROUP - 1, PART, 2 * RANK), BF16),
        pltpu.VMEM((GROUP - 1, PART, 2 * RANK), BF16),
        pltpu.SemaphoreType.DMA((n_remote,)),
        pltpu.SemaphoreType.DMA((n_remote,)),
        pltpu.SemaphoreType.DMA((3 + 3 * STEPS + 2,)),
    ]
    return pl.pallas_call(
        kernel,
        out_shape=(rows, rows, rows),
        in_specs=[any_space] * 4 + [pl.BlockSpec(memory_space=pltpu.SMEM)],
        out_specs=(vmem, any_space, any_space),
        scratch_shapes=scratch,
        compiler_params=pltpu.CompilerParams(
            collective_id=0, has_side_effects=True, vmem_limit_bytes=40 * 1024 * 1024
        ),
        name="train",
    )(tokens, master, moment, second, cube_bit)


def solution(mesh):
    in_specs = (
        P(None, "gossip", "fsdp", None),
        P("gossip", "fsdp", None),
        P("gossip", "fsdp", None),
        P("gossip", "fsdp", None),
        P(),
    )
    out_specs = (P("gossip", "fsdp", None), P("gossip", "fsdp", None), P("gossip", "fsdp", None))
    return jax.shard_map(body, mesh=mesh, in_specs=in_specs, out_specs=out_specs, check_vma=False)
```

```python
import math

import jax
import jax.numpy as jnp
from jax import lax
from jax.experimental import pallas as pl
from jax.experimental.pallas import tpu as pltpu
from jax.sharding import PartitionSpec as P

MESH = pl.DeviceIdType.MESH
F32, BF16 = jnp.float32, jnp.bfloat16

D = 5120
RANK = 128
STEPS = 2
DOC = 128
GROUP_TOK = 2048
ROWS = 320
CHIP_ROWS = 640
HALF = 2560
YS = 4
GROUP = 8
PART = 48
N_GROUPS = 46
N_LOCAL = 13
BULK = 12288
VMEM_LIMIT = 60 * 1024 * 1024
OTHERS = (1, 3, 2)


def part_start(member):
    return pl.multiple_of(16 * ((5 * member) // 2), 16)


def kernel(
    tokens, master, moment, second, cube, avg_out, mom_out, sec_out,
    weight, first, squares, wire, docs, xs, xt, xgram, pacc, gram_send, gram_recv, psend, prec, eall, right,
    keep_cross, keep_own, dsend, drec, zsend, zrec, grec, gsend, arec, averaged,
    bulk, send_sem, recv_sem, local_sem, near_sem, far_sem,
):
    f = lax.axis_index("fsdp")
    g = lax.axis_index("gossip")
    z, y, c = f // 8, (f // 2) % YS, f % 2
    q = g % GROUP

    def at(fi, gi):
        return {"fsdp": fi, "gossip": gi}

    def y_peer(k):
        return (y + k) % YS

    def y_dev(k):
        return at(z * 8 + y_peer(k) * 2 + c, g)

    core_dev = at(z * 8 + y * 2 + (1 - c), g)
    z_dev = at((1 - z) * 8 + y * 2 + c, g)

    def member(delta):
        bits = [(q // (1 << b)) % 2 for b in range(3)]
        return sum((1 - bits[b] if (delta >> b) & 1 else bits[b]) * (1 << b) for b in range(3))

    def gossip_dev(delta):
        return at(f, g - q + member(delta))

    barrier = pltpu.get_barrier_semaphore()

    def signal(sem, device):
        pl.semaphore_signal(sem, inc=1, device_id=device, device_id_type=MESH)

    for k in OTHERS:
        signal(barrier, at(z * 8 + y_peer(k) * 2, g))

    @pl.when(c == 1)
    def _():
        signal(barrier, core_dev)

    signal(barrier, at((1 - z) * 8 + y * 2 + 1, g))
    for delta in range(1, GROUP):
        signal(barrier, at(z * 8 + y * 2 + 1, g - q + member(delta)))

    def near_ready():
        @pl.when(c == 0)
        def _():
            pl.semaphore_wait(barrier, 2 * YS - 1)
            signal(near_sem, core_dev)

        @pl.when(c == 1)
        def _():
            pl.semaphore_wait(near_sem, 1)

    def far_ready():
        @pl.when(c == 1)
        def _():
            pl.semaphore_wait(barrier, 2 * GROUP)
            signal(far_sem, core_dev)

        @pl.when(c == 0)
        def _():
            pl.semaphore_wait(far_sem, 1)

    count = [0, 0]
    stage = [0]
    bytes_sent = [0] * (STEPS + 1)

    def new_group():
        count[0] += 1
        return count[0] - 1

    def remote(src, dst, device, group):
        pltpu.make_async_remote_copy(
            src_ref=src, dst_ref=dst, send_sem=send_sem.at[stage[0]], recv_sem=recv_sem.at[group],
            device_id=device, device_id_type=MESH,
        ).start()
        rows = math.prod(src.shape) // RANK
        bytes_sent[stage[0]] += rows

    def arrive(group, like):
        pltpu.make_async_remote_copy(
            src_ref=like, dst_ref=like, send_sem=send_sem.at[0], recv_sem=recv_sem.at[group],
            device_id=core_dev, device_id_type=MESH,
        ).wait_recv()

    def flush(which):
        like = bulk.at[pl.ds(0, bytes_sent[which]), :]
        pltpu.make_async_remote_copy(
            src_ref=like, dst_ref=like, send_sem=send_sem.at[which], recv_sem=recv_sem.at[0],
            device_id=core_dev, device_id_type=MESH,
        ).wait_send()
        bytes_sent[which] = 0

    def loaded(copy):
        copy.wait()

    def local(src, dst):
        i = count[1]
        count[1] += 1
        copy = pltpu.make_async_copy(src, dst, local_sem.at[i])
        copy.start()
        return copy

    def feature_cols(p, who):
        return pl.ds(pl.multiple_of(p * HALF + who * CHIP_ROWS, 128), CHIP_ROWS)

    def doc_rows(who):
        return pl.ds(pl.multiple_of(who * DOC, DOC), DOC)

    def rows_of(core):
        return pl.ds(pl.multiple_of(core * ROWS, 64), ROWS)

    def cols(h):
        return slice(h * RANK, (h + 1) * RANK)

    def dot(a, b):
        return jnp.dot(a, b, preferred_element_type=F32)

    def tdot(a, b):
        return lax.dot_general(a, b, (((0,), (0,)), ((), ())), preferred_element_type=F32)

    def send_tokens(s):
        groups = {}
        for k in OTHERS:
            groups[k] = new_group()
            for p in (0, 1):
                remote(
                    docs.at[s, :, feature_cols(p, y_peer(k))], xs.at[s, p, doc_rows(y), :], y_dev(k), groups[k]
                )
        return groups

    def send_weights(s, h):
        own = wire.at[s, h, z, rows_of(c), :]
        groups = new_group(), new_group()
        remote(own, own, z_dev, groups[0])
        remote(own, own, core_dev, groups[1])
        return groups

    def forward_weights(s, h):
        got = wire.at[s, h, 1 - z, rows_of(c), :]
        group = new_group()
        arrive(w_groups[h][0], got)
        remote(got, got, core_dev, group)
        return group

    def weights_here(group, s, h, p):
        arrive(group, wire.at[s, h, p, rows_of(1 - c), :])

    in_weight = local(master.at[0], weight)
    in_doc = [local(tokens.at[0, 0], docs.at[0])]
    loaded(in_weight)
    for h in (0, 1):
        wire[0, h, z, rows_of(c), :] = weight[:, cols(h)].astype(BF16)
    loaded(in_doc[0])
    near_ready()
    tok_groups = [send_tokens(0)]
    far_ready()
    w_groups = [send_weights(0, h) for h in (0, 1)]
    in_doc.append(local(tokens.at[1, 0], docs.at[1]))
    in_own = [
        [local(tokens.at[s, 0, :, feature_cols(p, y)], xs.at[s, p, doc_rows(y), :]) for p in (0, 1)]
        for s in range(STEPS)
    ]
    in_first = local(moment.at[0], first)
    in_squares = local(second.at[0], squares)

    m = D**-0.5
    r = RANK**-0.5
    alpha = (RANK / GROUP_TOK) ** 0.5
    tall = (DOC, RANK)

    def gram_of(s):
        x = docs[s]
        xgram[s] = lax.dot_general(x, x, (((1,), (1,)), ((), ())), preferred_element_type=F32)

    gram_of(0)

    for s in range(STEPS):

        def part_product(who, h, p):
            return dot(xs[s, p, doc_rows(who), :], wire[s, h, p])

        def part_gram(p):
            right[...] = wire[s, 1, p]
            return tdot(right[...], right[...])

        def tokens_here(k):
            arrive(tok_groups[s][k], xs.at[s, :, doc_rows((y + YS - k) % YS), :])

        gram_group, p_groups = new_group(), (new_group(), new_group())

        def send_gram(gram):
            gram_send[s] = gram.astype(BF16)
            for k in OTHERS:
                remote(gram_send.at[s], gram_recv.at[s, k - 1], y_dev(k), gram_group)

        def send_product(k, h, value):
            psend[s, h, k - 1] = value.astype(BF16)
            remote(psend.at[s, h, k - 1], prec.at[s, h, k - 1], y_dev(k), p_groups[h])

        if s == 0:
            forwards = [forward_weights(s, h) for h in (0, 1)]
            for h in (0, 1):
                weights_here(w_groups[h][1], s, h, z)
                weights_here(forwards[h], s, h, 1 - z)
            gram = part_gram(0) + part_gram(1)
            send_gram(gram)
            for copy in in_own[s]:
                loaded(copy)
            for k in OTHERS:
                tokens_here(YS - k)
                for h in (0, 1):
                    send_product(k, h, part_product(y_peer(k), h, 0) + part_product(y_peer(k), h, 1))
            for h in (0, 1):
                pacc[h, 0] = part_product(y, h, 0) + part_product(y, h, 1)
        else:
            for copy in in_own[s]:
                loaded(copy)
            for k in OTHERS:
                tokens_here(k)
            weights_here(w_groups[0][1], s, 0, z)
            for k in range(YS):
                pacc[0, k] = part_product(y_peer(k), 0, z)
            weights_here(forward_weights(s, 0), s, 0, 1 - z)
            for k in OTHERS:
                send_product(k, 0, pacc[0, k] + part_product(y_peer(k), 0, 1 - z))
            pacc[0, 0] += part_product(y, 0, 1 - z)
            weights_here(w_groups[1][1], s, 1, z)
            for k in range(YS):
                pacc[1, k] = part_product(y_peer(k), 1, z)
            gram = part_gram(z)
            weights_here(forward_weights(s, 1), s, 1, 1 - z)
            gram += part_gram(1 - z)
            send_gram(gram)
            for k in OTHERS:
                send_product(k, 1, pacc[1, k] + part_product(y_peer(k), 1, 1 - z))
            pacc[1, 0] += part_product(y, 1, 1 - z)

        for p in (0, 1):
            xt[p] = xs[s, p].T
        at_t = lax.broadcasted_iota(jnp.int32, tall, 0)
        at_j = lax.broadcasted_iota(jnp.int32, tall, 1)
        xx = xgram[s]
        sx = jnp.sum(jnp.where(at_j == at_t, xx, 0.0), axis=1, keepdims=True)
        xn = jnp.sum(jnp.where(at_j == at_t + 1, xx, 0.0), axis=1, keepdims=True)
        ix = lax.rsqrt(sx * (1.0 / D) + 1e-5)
        ixn = pltpu.roll(jnp.broadcast_to(ix, tall), DOC - 1, 0)[:, :1]
        kept = jnp.where(lax.broadcasted_iota(jnp.int32, (DOC, 1), 0) == DOC - 1, 0.0, alpha)

        arrive(gram_group, gram_recv.at[s])
        for k in range(3):
            gram += gram_recv[s, k].astype(F32)
        ghi = gram.astype(BF16)
        glo = (gram - ghi.astype(F32)).astype(BF16)
        arrive(p_groups[0], prec.at[s, 0])
        left = pacc[0, 0]
        for k in range(3):
            left += prec[s, 0, k].astype(F32)
        low = (ix * left * m).astype(BF16)
        lowf = low.astype(F32)
        lowg = dot(low, ghi) + dot(low, glo)
        arrive(p_groups[1], prec.at[s, 1])
        pr = pacc[1, 0]
        for k in range(3):
            pr += prec[s, 1, k].astype(F32)

        prn = pltpu.roll(pr, DOC - 1, 0)
        oo = (
            sx
            + (2 * r) * jnp.sum(lowf * pr, axis=1, keepdims=True)
            + (r * r) * jnp.sum(lowf * lowg, axis=1, keepdims=True)
        )
        inv = lax.rsqrt(oo * (1.0 / D) + 1e-5)
        sno = ixn * (xn + r * jnp.sum(lowf * prn, axis=1, keepdims=True))
        cc = kept * (inv * inv * oo - inv * sno) * (1.0 / D)
        aa = inv * inv * (kept - cc)
        bb = kept * inv * ixn
        dlow = (aa * (pr + r * lowg) - bb * prn) * (RANK * D) ** -0.5
        e_groups = []

        def send_factor(kind, value):
            eall[s, kind, y] = value.astype(BF16)
            e_groups.append(new_group())
            for k in OTHERS:
                remote(eall.at[s, kind, y], eall.at[s, kind, y], y_dev(k), e_groups[kind])

        send_factor(0, ix * dlow)
        al = aa * lowf
        send_factor(1, r * (al - pltpu.roll(bb * lowf, 1, 0)))
        send_factor(2, (r * r) * tdot(low, al.astype(BF16)))
        if s + 1 < STEPS:
            stage[0] = s + 1
            loaded(in_doc[s + 1])
            tok_groups.append(send_tokens(s + 1))

        own_groups = []
        z_groups = []
        for h in (0, 1):
            for kind in (0,) if h == 0 else (1, 2):
                arrive(e_groups[kind], eall.at[s, kind, pl.ds(0, YS - 1)])
            factor = eall[s, h].reshape(YS * DOC, RANK)
            if h == 1:
                outer = sum(eall[s, 2, j].astype(F32) for j in range(YS)).astype(BF16)

            def gradient(p, core):
                rows = dot(xt[p, rows_of(core), :], factor)
                if h == 1:
                    rows += dot(wire[s, 1, p, rows_of(core), :], outer)
                return rows

            dsend[s, h, 0] = gradient(1 - z, 1 - c).astype(BF16)
            cross = new_group()
            remote(dsend.at[s, h, 0], drec.at[s, h, 0], core_dev, cross)
            keep_cross[...] = gradient(1 - z, c)
            dsend[s, h, 1] = gradient(z, 1 - c).astype(BF16)
            own_groups.append(new_group())
            remote(dsend.at[s, h, 1], drec.at[s, h, 1], core_dev, own_groups[h])
            arrive(cross, drec.at[s, h, 0])
            zsend[s, h] = (keep_cross[...] + drec[s, h, 0].astype(F32)).astype(BF16)
            z_groups.append(new_group())
            remote(zsend.at[s, h], zrec.at[s, h], z_dev, z_groups[h])
            keep_own[h] = gradient(z, c)
        if s == 0:
            loaded(in_first)
            loaded(in_squares)
            gram_of(1)
        for h in (0, 1):
            arrive(own_groups[h], drec.at[s, h, 1])
            keep_own[h] += drec[s, h, 1].astype(F32)
        w_groups = []
        g_groups = []
        if s + 1 == STEPS:
            stage[0] = STEPS
        for h in (0, 1):
            arrive(z_groups[h], zrec.at[s, h])
            grad = keep_own[h] + zrec[s, h].astype(F32)
            one = 0.9 * first[:, cols(h)] + 0.1 * grad
            two = 0.95 * squares[:, cols(h)] + 0.05 * grad * grad
            new = weight[:, cols(h)] - 0.02 * one / (jnp.sqrt(two) + 1e-8)
            first[:, cols(h)] = one
            squares[:, cols(h)] = two
            weight[:, cols(h)] = new
            wire[s + 1, h, z, rows_of(c), :] = new.astype(BF16)
            if s + 1 < STEPS:
                w_groups.append(send_weights(s + 1, h))
                continue
            g_groups.append(new_group())
            for delta in range(1, GROUP):
                start = c * ROWS + part_start(member(delta))
                rows = pl.ds(pl.multiple_of(start, 16), PART)
                remote(wire.at[STEPS, h, z, rows, :], grec.at[h, delta - 1], gossip_dev(delta), g_groups[h])

    outs = [local(first, mom_out.at[0]), local(squares, sec_out.at[0])]
    share = []
    for b in range(3):
        used = sum((cube[i] == b).astype(jnp.int32) for i in range(4))
        share.append(0.5 * jnp.minimum(used, 1).astype(F32))
    a_groups = []
    for h in (0, 1):
        held = [weight[pl.ds(part_start(q), PART), cols(h)]]
        arrive(g_groups[h], grec.at[h])
        for delta in range(1, GROUP):
            held.append(grec[h, delta - 1].astype(F32))
        for b in range(3):
            held = [held[d] + share[b] * (held[d ^ (1 << b)] - held[d]) for d in range(GROUP)]
        a_groups.append(new_group())
        for delta in range(1, GROUP):
            gsend[h, delta - 1] = held[delta].astype(BF16)
            remote(gsend.at[h, delta - 1], arec.at[h, delta - 1], gossip_dev(delta), a_groups[h])
        averaged[h, pl.ds(part_start(q), PART), :] = held[0]
    for which in range(STEPS):
        flush(which)
    for h in (0, 1):
        arrive(a_groups[h], arec.at[h])
        for delta in range(1, GROUP):
            averaged[h, pl.ds(part_start(member(delta)), PART), :] = arec[h, delta - 1].astype(F32)
        outs.append(local(averaged.at[h], avg_out.at[0, :, cols(h)]))

    flush(STEPS)
    for copy in outs:
        loaded(copy)


def store_kernel(*refs):
    ins, outs, held, sems = refs[:3], refs[3:6], refs[6:9], refs[9]
    reads = [pltpu.make_async_copy(ins[i], held[i], sems.at[i]) for i in range(3)]
    writes = [pltpu.make_async_copy(held[i], outs[i], sems.at[3 + i]) for i in range(3)]
    for copy in reads:
        copy.start()
    for i in range(3):
        reads[i].wait()
        writes[i].start()
    for copy in writes:
        copy.wait()


def body(tokens, master, moment, second, cube_bit):
    any_space = pl.BlockSpec(memory_space=pl.ANY)
    rows = jax.ShapeDtypeStruct((1, ROWS, 2 * RANK), F32)
    scratch = [
        pltpu.VMEM((ROWS, 2 * RANK), F32),
        pltpu.VMEM((ROWS, 2 * RANK), F32),
        pltpu.VMEM((ROWS, 2 * RANK), F32),
        pltpu.VMEM((STEPS + 1, 2, 2, CHIP_ROWS, RANK), BF16),
        pltpu.VMEM((STEPS, DOC, D), BF16),
        pltpu.VMEM((STEPS, 2, YS * DOC, CHIP_ROWS), BF16),
        pltpu.VMEM((2, CHIP_ROWS, YS * DOC), BF16),
        pltpu.VMEM((STEPS, DOC, DOC), F32),
        pltpu.VMEM((2, YS, DOC, RANK), F32),
        pltpu.VMEM((STEPS, RANK, RANK), BF16),
        pltpu.VMEM((STEPS, 3, RANK, RANK), BF16),
        pltpu.VMEM((STEPS, 2, 3, DOC, RANK), BF16),
        pltpu.VMEM((STEPS, 2, 3, DOC, RANK), BF16),
        pltpu.VMEM((STEPS, 3, YS, DOC, RANK), BF16),
        pltpu.VMEM((CHIP_ROWS, RANK), BF16),
        pltpu.VMEM((ROWS, RANK), F32),
        pltpu.VMEM((2, ROWS, RANK), F32),
        pltpu.VMEM((STEPS, 2, 2, ROWS, RANK), BF16),
        pltpu.VMEM((STEPS, 2, 2, ROWS, RANK), BF16),
        pltpu.VMEM((STEPS, 2, ROWS, RANK), BF16),
        pltpu.VMEM((STEPS, 2, ROWS, RANK), BF16),
        pltpu.VMEM((2, GROUP - 1, PART, RANK), BF16),
        pltpu.VMEM((2, GROUP - 1, PART, RANK), BF16),
        pltpu.VMEM((2, GROUP - 1, PART, RANK), BF16),
        pltpu.VMEM((2, ROWS, RANK), F32),
        pltpu.VMEM((BULK, RANK), BF16),
        pltpu.SemaphoreType.DMA((STEPS + 1,)),
        pltpu.SemaphoreType.DMA((N_GROUPS,)),
        pltpu.SemaphoreType.DMA((N_LOCAL,)),
        pltpu.SemaphoreType.REGULAR,
        pltpu.SemaphoreType.REGULAR,
    ]
    outs = pl.pallas_call(
        kernel,
        out_shape=(rows, rows, rows),
        in_specs=[any_space] * 4 + [pl.BlockSpec(memory_space=pltpu.SMEM)],
        out_specs=(any_space,) * 3,
        scratch_shapes=scratch,
        compiler_params=pltpu.CompilerParams(
            collective_id=0, has_side_effects=True, vmem_limit_bytes=VMEM_LIMIT
        ),
        name="train",
    )(tokens, master, moment, second, cube_bit)
    return pl.pallas_call(
        store_kernel,
        out_shape=(rows, rows, rows),
        in_specs=[any_space] * 3,
        out_specs=(any_space,) * 3,
        scratch_shapes=[pltpu.VMEM((1, ROWS, 2 * RANK), F32)] * 3 + [pltpu.SemaphoreType.DMA((6,))],
        compiler_params=pltpu.CompilerParams(vmem_limit_bytes=VMEM_LIMIT),
        name="store",
    )(*outs)


def solution(mesh):
    in_specs = (
        P(None, "gossip", "fsdp", None),
        P("gossip", "fsdp", None),
        P("gossip", "fsdp", None),
        P("gossip", "fsdp", None),
        P(),
    )
    out_specs = (P("gossip", "fsdp", None), P("gossip", "fsdp", None), P("gossip", "fsdp", None))
    return jax.shard_map(body, mesh=mesh, in_specs=in_specs, out_specs=out_specs, check_vma=False)
```

```python
import math

import jax
import jax.numpy as jnp
from jax import lax
from jax.experimental import pallas as pl
from jax.experimental.pallas import tpu as pltpu
from jax.sharding import PartitionSpec as P

MESH = pl.DeviceIdType.MESH
F32, BF16 = jnp.float32, jnp.bfloat16

D = 5120
RANK = 128
STEPS = 2
DOC = 128
GROUP_TOK = 2048
ROWS = 320
CHIP_ROWS = 640
HALF = 2560
YS = 4
GROUP = 8
PART = 48
N_GROUPS = 47
N_LOCAL = 13
BULK = 12288
VMEM_LIMIT = 60 * 1024 * 1024
OTHERS = (1, 3, 2)


def part_start(member):
    return pl.multiple_of(16 * ((5 * member) // 2), 16)


def kernel(
    tokens, master, moment, second, cube, avg_out, mom_out, sec_out,
    weight, first, squares, wire, docs, xs, xt, xgram, pacc, wide, gram_send, gram_recv, half_send, half_recv, psend, prec, eall, right,
    keep_cross, keep_own, dsend, drec, zsend, zrec, grec, gsend, arec, averaged,
    bulk, send_sem, recv_sem, local_sem, near_sem, far_sem,
):
    f = lax.axis_index("fsdp")
    g = lax.axis_index("gossip")
    z, y, c = f // 8, (f // 2) % YS, f % 2
    q = g % GROUP

    def at(fi, gi):
        return {"fsdp": fi, "gossip": gi}

    def y_peer(k):
        return (y + k) % YS

    def y_dev(k):
        return at(z * 8 + y_peer(k) * 2 + c, g)

    core_dev = at(z * 8 + y * 2 + (1 - c), g)
    z_dev = at((1 - z) * 8 + y * 2 + c, g)

    def member(delta):
        bits = [(q // (1 << b)) % 2 for b in range(3)]
        return sum((1 - bits[b] if (delta >> b) & 1 else bits[b]) * (1 << b) for b in range(3))

    def gossip_dev(delta):
        return at(f, g - q + member(delta))

    barrier = pltpu.get_barrier_semaphore()

    def signal(sem, device):
        pl.semaphore_signal(sem, inc=1, device_id=device, device_id_type=MESH)

    for k in OTHERS:
        signal(barrier, at(z * 8 + y_peer(k) * 2, g))

    @pl.when(c == 1)
    def _():
        signal(barrier, core_dev)

    signal(barrier, at((1 - z) * 8 + y * 2 + 1, g))
    for delta in range(1, GROUP):
        signal(barrier, at(z * 8 + y * 2 + 1, g - q + member(delta)))

    def near_ready():
        @pl.when(c == 0)
        def _():
            pl.semaphore_wait(barrier, 2 * YS - 1)
            signal(near_sem, core_dev)

        @pl.when(c == 1)
        def _():
            pl.semaphore_wait(near_sem, 1)

    def far_ready():
        @pl.when(c == 1)
        def _():
            pl.semaphore_wait(barrier, 2 * GROUP)
            signal(far_sem, core_dev)

        @pl.when(c == 0)
        def _():
            pl.semaphore_wait(far_sem, 1)

    count = [0, 0]
    stage = [0]
    bytes_sent = [0] * (STEPS + 1)

    def new_group():
        count[0] += 1
        return count[0] - 1

    def remote(src, dst, device, group):
        pltpu.make_async_remote_copy(
            src_ref=src, dst_ref=dst, send_sem=send_sem.at[stage[0]], recv_sem=recv_sem.at[group],
            device_id=device, device_id_type=MESH,
        ).start()
        rows = math.prod(src.shape) // RANK
        bytes_sent[stage[0]] += rows

    def arrive(group, like):
        pltpu.make_async_remote_copy(
            src_ref=like, dst_ref=like, send_sem=send_sem.at[0], recv_sem=recv_sem.at[group],
            device_id=core_dev, device_id_type=MESH,
        ).wait_recv()

    def flush(which):
        like = bulk.at[pl.ds(0, bytes_sent[which]), :]
        pltpu.make_async_remote_copy(
            src_ref=like, dst_ref=like, send_sem=send_sem.at[which], recv_sem=recv_sem.at[0],
            device_id=core_dev, device_id_type=MESH,
        ).wait_send()
        bytes_sent[which] = 0

    def loaded(copy):
        copy.wait()

    def local(src, dst):
        i = count[1]
        count[1] += 1
        copy = pltpu.make_async_copy(src, dst, local_sem.at[i])
        copy.start()
        return copy

    def feature_cols(p, who):
        return pl.ds(pl.multiple_of(p * HALF + who * CHIP_ROWS, 128), CHIP_ROWS)

    def doc_rows(who):
        return pl.ds(pl.multiple_of(who * DOC, DOC), DOC)

    def rows_of(core):
        return pl.ds(pl.multiple_of(core * ROWS, 64), ROWS)

    def cols(h):
        return slice(h * RANK, (h + 1) * RANK)

    def dot(a, b):
        return jnp.dot(a, b, preferred_element_type=F32)

    def tdot(a, b):
        return lax.dot_general(a, b, (((0,), (0,)), ((), ())), preferred_element_type=F32)

    def send_tokens(s):
        groups = {k: new_group() for k in OTHERS}
        for k, p in ((1, 0), (3, 0), (1, 1), (3, 1), (2, 0), (2, 1)):
            remote(docs.at[s, :, feature_cols(p, y_peer(k))], xs.at[s, p, doc_rows(y), :], y_dev(k), groups[k])
        return groups

    def send_weights(s, h):
        own = wire.at[s, h, z, rows_of(c), :]
        groups = new_group(), new_group()
        remote(own, own, z_dev, groups[0])
        remote(own, own, core_dev, groups[1])
        return groups

    def forward_weights(s, h):
        got = wire.at[s, h, 1 - z, rows_of(c), :]
        group = new_group()
        arrive(w_groups[h][0], got)
        remote(got, got, core_dev, group)
        return group

    def weights_here(group, s, h, p):
        arrive(group, wire.at[s, h, p, rows_of(1 - c), :])

    in_weight = local(master.at[0], weight)
    in_doc = [local(tokens.at[0, 0], docs.at[0])]
    loaded(in_weight)
    for h in (0, 1):
        wire[0, h, z, rows_of(c), :] = weight[:, cols(h)].astype(BF16)
    loaded(in_doc[0])
    near_ready()
    tok_groups = [send_tokens(0)]
    far_ready()
    w_groups = [send_weights(0, h) for h in (0, 1)]
    in_doc.append(local(tokens.at[1, 0], docs.at[1]))
    in_own = [
        [local(tokens.at[s, 0, :, feature_cols(p, y)], xs.at[s, p, doc_rows(y), :]) for p in (0, 1)]
        for s in range(STEPS)
    ]
    in_first = local(moment.at[0], first)
    in_squares = local(second.at[0], squares)

    m = D**-0.5
    r = RANK**-0.5
    alpha = (RANK / GROUP_TOK) ** 0.5
    tall = (DOC, RANK)

    def gram_of(s):
        x = docs[s]
        xgram[s] = lax.dot_general(x, x, (((1,), (1,)), ((), ())), preferred_element_type=F32)

    gram_of(0)

    for s in range(STEPS):

        def part_product(who, h, p):
            return dot(xs[s, p, doc_rows(who), :], wire[s, h, p])

        def part_gram(p, core):
            right[...] = wire[s, 1, p, rows_of(core), :]
            return tdot(right[...], right[...])

        def tokens_here(k):
            arrive(tok_groups[s][k], xs.at[s, :, doc_rows((y + YS - k) % YS), :])

        gram_group, p_groups = new_group(), (new_group(), new_group())

        def send_gram(gram):
            gram_send[s] = gram.astype(BF16)
            for k in OTHERS:
                remote(gram_send.at[s], gram_recv.at[s, k - 1], y_dev(k), gram_group)

        def gram_sum(gram):
            arrive(gram_group, gram_recv.at[s])
            for k in range(3):
                gram += gram_recv[s, k].astype(F32)
            return gram

        def send_product(k, h, value):
            psend[s, h, k - 1] = value.astype(BF16)
            remote(psend.at[s, h, k - 1], prec.at[s, h, k - 1], y_dev(k), p_groups[h])

        if s == 0:
            forwards = [forward_weights(s, h) for h in (0, 1)]
            for h in (0, 1):
                weights_here(w_groups[h][1], s, h, z)
                weights_here(forwards[h], s, h, 1 - z)
            gram = sum(part_gram(p, core) for p in (0, 1) for core in (0, 1))
            send_gram(gram)
            for copy in in_own[s]:
                loaded(copy)
            for p in (0, 1):
                wide[p] = jnp.concatenate([wire[s, 0, p], wire[s, 1, p]], axis=1)

            def whole_product(who):
                return sum(dot(xs[s, p, doc_rows(who), :], wide[p]) for p in (0, 1))

            for k in OTHERS:
                tokens_here(YS - k)
                value = whole_product(y_peer(k))
                for h in (0, 1):
                    send_product(k, h, value[:, cols(h)])
            value = whole_product(y)
            for h in (0, 1):
                pacc[h, 0] = value[:, cols(h)]
        else:
            for copy in in_own[s]:
                loaded(copy)
            for k in OTHERS:
                tokens_here(k)
            weights_here(w_groups[1][1], s, 1, z)
            gram = part_gram(z, c) + part_gram(z, 1 - c)
            send_gram(gram)
            weights_here(w_groups[0][1], s, 0, z)
            for k in range(YS):
                pacc[0, k] = part_product(y_peer(k), 0, z)
                pacc[1, k] = part_product(y_peer(k), 1, z)
            forward = forward_weights(s, 0)
            gram = gram_sum(gram)
            half_send[...] = gram.astype(BF16)
            half_group = new_group()
            remote(half_send, half_recv, z_dev, half_group)
            weights_here(forward, s, 0, 1 - z)
            for k in OTHERS:
                send_product(k, 0, pacc[0, k] + part_product(y_peer(k), 0, 1 - z))
            pacc[0, 0] += part_product(y, 0, 1 - z)
            forward = forward_weights(s, 1)
            weights_here(forward, s, 1, 1 - z)
            for k in OTHERS:
                send_product(k, 1, pacc[1, k] + part_product(y_peer(k), 1, 1 - z))
            pacc[1, 0] += part_product(y, 1, 1 - z)

        for p in (0, 1):
            xt[p] = xs[s, p].T
        at_t = lax.broadcasted_iota(jnp.int32, tall, 0)
        at_j = lax.broadcasted_iota(jnp.int32, tall, 1)
        xx = xgram[s]
        sx = jnp.sum(jnp.where(at_j == at_t, xx, 0.0), axis=1, keepdims=True)
        xn = jnp.sum(jnp.where(at_j == at_t + 1, xx, 0.0), axis=1, keepdims=True)
        ix = lax.rsqrt(sx * (1.0 / D) + 1e-5)
        ixn = pltpu.roll(jnp.broadcast_to(ix, tall), DOC - 1, 0)[:, :1]
        kept = jnp.where(lax.broadcasted_iota(jnp.int32, (DOC, 1), 0) == DOC - 1, 0.0, alpha)

        if s == 0:
            gram = gram_sum(gram)
        else:
            arrive(half_group, half_recv)
            gram += half_recv[...].astype(F32)
        ghi = gram.astype(BF16)
        glo = (gram - ghi.astype(F32)).astype(BF16)
        arrive(p_groups[0], prec.at[s, 0])
        left = pacc[0, 0]
        for k in range(3):
            left += prec[s, 0, k].astype(F32)
        low = (ix * left * m).astype(BF16)
        lowf = low.astype(F32)
        lowg = dot(low, ghi) + dot(low, glo)
        arrive(p_groups[1], prec.at[s, 1])
        pr = pacc[1, 0]
        for k in range(3):
            pr += prec[s, 1, k].astype(F32)

        prn = pltpu.roll(pr, DOC - 1, 0)
        oo = (
            sx
            + (2 * r) * jnp.sum(lowf * pr, axis=1, keepdims=True)
            + (r * r) * jnp.sum(lowf * lowg, axis=1, keepdims=True)
        )
        inv = lax.rsqrt(oo * (1.0 / D) + 1e-5)
        sno = ixn * (xn + r * jnp.sum(lowf * prn, axis=1, keepdims=True))
        cc = kept * (inv * inv * oo - inv * sno) * (1.0 / D)
        aa = inv * inv * (kept - cc)
        bb = kept * inv * ixn
        dlow = (aa * (pr + r * lowg) - bb * prn) * (RANK * D) ** -0.5
        e_groups = []

        def send_factor(kind, value):
            eall[s, kind, y] = value.astype(BF16)
            e_groups.append(new_group())
            for k in OTHERS:
                remote(eall.at[s, kind, y], eall.at[s, kind, y], y_dev(k), e_groups[kind])

        send_factor(0, ix * dlow)
        al = aa * lowf
        send_factor(1, r * (al - pltpu.roll(bb * lowf, 1, 0)))
        send_factor(2, (r * r) * tdot(low, al.astype(BF16)))
        if s + 1 < STEPS:
            stage[0] = s + 1
            loaded(in_doc[s + 1])
            tok_groups.append(send_tokens(s + 1))
        own_groups = []
        z_groups = []
        for h in (0, 1):
            for kind in (0,) if h == 0 else (1, 2):
                arrive(e_groups[kind], eall.at[s, kind, pl.ds(0, YS - 1)])
            factor = eall[s, h].reshape(YS * DOC, RANK)
            if h == 1:
                outer = sum(eall[s, 2, j].astype(F32) for j in range(YS)).astype(BF16)

            def gradient(p, core):
                rows = dot(xt[p, rows_of(core), :], factor)
                if h == 1:
                    rows += dot(wire[s, 1, p, rows_of(core), :], outer)
                return rows

            dsend[s, h, 0] = gradient(1 - z, 1 - c).astype(BF16)
            cross = new_group()
            remote(dsend.at[s, h, 0], drec.at[s, h, 0], core_dev, cross)
            keep_cross[...] = gradient(1 - z, c)
            dsend[s, h, 1] = gradient(z, 1 - c).astype(BF16)
            own_groups.append(new_group())
            remote(dsend.at[s, h, 1], drec.at[s, h, 1], core_dev, own_groups[h])
            arrive(cross, drec.at[s, h, 0])
            zsend[s, h] = (keep_cross[...] + drec[s, h, 0].astype(F32)).astype(BF16)
            z_groups.append(new_group())
            remote(zsend.at[s, h], zrec.at[s, h], z_dev, z_groups[h])
            keep_own[h] = gradient(z, c)
        if s == 0:
            loaded(in_first)
            loaded(in_squares)
            gram_of(1)
        for h in (0, 1):
            arrive(own_groups[h], drec.at[s, h, 1])
            keep_own[h] += drec[s, h, 1].astype(F32)
        w_groups = []
        g_groups = []
        if s + 1 == STEPS:
            stage[0] = STEPS
        for h in (0, 1):
            arrive(z_groups[h], zrec.at[s, h])
            grad = keep_own[h] + zrec[s, h].astype(F32)
            one = 0.9 * first[:, cols(h)] + 0.1 * grad
            two = 0.95 * squares[:, cols(h)] + 0.05 * grad * grad
            new = weight[:, cols(h)] - 0.02 * one / (jnp.sqrt(two) + 1e-8)
            first[:, cols(h)] = one
            squares[:, cols(h)] = two
            weight[:, cols(h)] = new
            wire[s + 1, h, z, rows_of(c), :] = new.astype(BF16)
            if s + 1 < STEPS:
                w_groups.append(send_weights(s + 1, h))
                continue
            g_groups.append(new_group())
            for delta in range(1, GROUP):
                start = c * ROWS + part_start(member(delta))
                rows = pl.ds(pl.multiple_of(start, 16), PART)
                remote(wire.at[STEPS, h, z, rows, :], grec.at[h, delta - 1], gossip_dev(delta), g_groups[h])

    outs = [local(first, mom_out.at[0]), local(squares, sec_out.at[0])]
    share = []
    for b in range(3):
        used = sum((cube[i] == b).astype(jnp.int32) for i in range(4))
        share.append(0.5 * jnp.minimum(used, 1).astype(F32))
    a_groups = []
    for h in (0, 1):
        held = [weight[pl.ds(part_start(q), PART), cols(h)]]
        arrive(g_groups[h], grec.at[h])
        for delta in range(1, GROUP):
            held.append(grec[h, delta - 1].astype(F32))
        for b in range(3):
            held = [held[d] + share[b] * (held[d ^ (1 << b)] - held[d]) for d in range(GROUP)]
        a_groups.append(new_group())
        for delta in range(1, GROUP):
            gsend[h, delta - 1] = held[delta].astype(BF16)
            remote(gsend.at[h, delta - 1], arec.at[h, delta - 1], gossip_dev(delta), a_groups[h])
        averaged[h, pl.ds(part_start(q), PART), :] = held[0]
    for which in range(STEPS):
        flush(which)
    for h in (0, 1):
        arrive(a_groups[h], arec.at[h])
        for delta in range(1, GROUP):
            averaged[h, pl.ds(part_start(member(delta)), PART), :] = arec[h, delta - 1].astype(F32)
        outs.append(local(averaged.at[h], avg_out.at[0, :, cols(h)]))

    flush(STEPS)
    for copy in outs:
        loaded(copy)


def store_kernel(*refs):
    ins, outs, held, sems = refs[:3], refs[3:6], refs[6:9], refs[9]
    reads = [pltpu.make_async_copy(ins[i], held[i], sems.at[i]) for i in range(3)]
    writes = [pltpu.make_async_copy(held[i], outs[i], sems.at[3 + i]) for i in range(3)]
    for copy in reads:
        copy.start()
    for i in range(3):
        reads[i].wait()
        writes[i].start()
    for copy in writes:
        copy.wait()


def body(tokens, master, moment, second, cube_bit):
    any_space = pl.BlockSpec(memory_space=pl.ANY)
    rows = jax.ShapeDtypeStruct((1, ROWS, 2 * RANK), F32)
    scratch = [
        pltpu.VMEM((ROWS, 2 * RANK), F32),
        pltpu.VMEM((ROWS, 2 * RANK), F32),
        pltpu.VMEM((ROWS, 2 * RANK), F32),
        pltpu.VMEM((STEPS + 1, 2, 2, CHIP_ROWS, RANK), BF16),
        pltpu.VMEM((STEPS, DOC, D), BF16),
        pltpu.VMEM((STEPS, 2, YS * DOC, CHIP_ROWS), BF16),
        pltpu.VMEM((2, CHIP_ROWS, YS * DOC), BF16),
        pltpu.VMEM((STEPS, DOC, DOC), F32),
        pltpu.VMEM((2, YS, DOC, RANK), F32),
        pltpu.VMEM((2, CHIP_ROWS, 2 * RANK), BF16),
        pltpu.VMEM((STEPS, RANK, RANK), BF16),
        pltpu.VMEM((STEPS, 3, RANK, RANK), BF16),
        pltpu.VMEM((RANK, RANK), BF16),
        pltpu.VMEM((RANK, RANK), BF16),
        pltpu.VMEM((STEPS, 2, 3, DOC, RANK), BF16),
        pltpu.VMEM((STEPS, 2, 3, DOC, RANK), BF16),
        pltpu.VMEM((STEPS, 3, YS, DOC, RANK), BF16),
        pltpu.VMEM((ROWS, RANK), BF16),
        pltpu.VMEM((ROWS, RANK), F32),
        pltpu.VMEM((2, ROWS, RANK), F32),
        pltpu.VMEM((STEPS, 2, 2, ROWS, RANK), BF16),
        pltpu.VMEM((STEPS, 2, 2, ROWS, RANK), BF16),
        pltpu.VMEM((STEPS, 2, ROWS, RANK), BF16),
        pltpu.VMEM((STEPS, 2, ROWS, RANK), BF16),
        pltpu.VMEM((2, GROUP - 1, PART, RANK), BF16),
        pltpu.VMEM((2, GROUP - 1, PART, RANK), BF16),
        pltpu.VMEM((2, GROUP - 1, PART, RANK), BF16),
        pltpu.VMEM((2, ROWS, RANK), F32),
        pltpu.VMEM((BULK, RANK), BF16),
        pltpu.SemaphoreType.DMA((STEPS + 1,)),
        pltpu.SemaphoreType.DMA((N_GROUPS,)),
        pltpu.SemaphoreType.DMA((N_LOCAL,)),
        pltpu.SemaphoreType.REGULAR,
        pltpu.SemaphoreType.REGULAR,
    ]
    outs = pl.pallas_call(
        kernel,
        out_shape=(rows, rows, rows),
        in_specs=[any_space] * 4 + [pl.BlockSpec(memory_space=pltpu.SMEM)],
        out_specs=(any_space,) * 3,
        scratch_shapes=scratch,
        compiler_params=pltpu.CompilerParams(
            collective_id=0, has_side_effects=True, vmem_limit_bytes=VMEM_LIMIT
        ),
        name="train",
    )(tokens, master, moment, second, cube_bit)
    return pl.pallas_call(
        store_kernel,
        out_shape=(rows, rows, rows),
        in_specs=[any_space] * 3,
        out_specs=(any_space,) * 3,
        scratch_shapes=[pltpu.VMEM((1, ROWS, 2 * RANK), F32)] * 3 + [pltpu.SemaphoreType.DMA((6,))],
        compiler_params=pltpu.CompilerParams(vmem_limit_bytes=VMEM_LIMIT),
        name="store",
    )(*outs)


def solution(mesh):
    in_specs = (
        P(None, "gossip", "fsdp", None),
        P("gossip", "fsdp", None),
        P("gossip", "fsdp", None),
        P("gossip", "fsdp", None),
        P(),
    )
    out_specs = (P("gossip", "fsdp", None), P("gossip", "fsdp", None), P("gossip", "fsdp", None))
    return jax.shard_map(body, mesh=mesh, in_specs=in_specs, out_specs=out_specs, check_vma=False)
```

```python
import math

import jax
import jax.numpy as jnp
from jax import lax
from jax.experimental import pallas as pl
from jax.experimental.pallas import tpu as pltpu
from jax.sharding import PartitionSpec as P

MESH = pl.DeviceIdType.MESH
F32, BF16 = jnp.float32, jnp.bfloat16

D = 5120
RANK = 128
STEPS = 2
DOC = 128
GROUP_TOK = 2048
ROWS = 320
CHIP_ROWS = 640
HALF = 2560
YS = 4
GROUP = 8
PART = 48
N_GROUPS = 27
N_LOCAL = 13
BULK = 12288
VMEM_LIMIT = 60 * 1024 * 1024
OTHERS = (1, 3, 2)


def part_start(member):
    return pl.multiple_of(16 * ((5 * member) // 2), 16)


def kernel(
    tokens, master, moment, second, cube, avg_out, mom_out, sec_out,
    weight, first, squares, wire, docs, xs, xt, xgram, pacc, wide, gram_send, gram_recv, half_send, half_recv,
    gram_full, core_gram_send, core_gram_recv, psend, prec, eall, right,
    keep_cross, keep_own, dsend, drec, zsend, zrec, grec, gsend, arec, averaged,
    bulk, send_sem, recv_sem, local_sem, near_sem, far_sem,
):
    f = lax.axis_index("fsdp")
    g = lax.axis_index("gossip")
    z, y, c = f // 8, (f // 2) % YS, f % 2
    q = g % GROUP

    def at(fi, gi):
        return {"fsdp": fi, "gossip": gi}

    def y_peer(k):
        return (y + k) % YS

    def y_dev(k):
        return at(z * 8 + y_peer(k) * 2 + c, g)

    core_dev = at(z * 8 + y * 2 + (1 - c), g)
    z_dev = at((1 - z) * 8 + y * 2 + c, g)

    def member(delta):
        bits = [(q // (1 << b)) % 2 for b in range(3)]
        return sum((1 - bits[b] if (delta >> b) & 1 else bits[b]) * (1 << b) for b in range(3))

    def gossip_dev(delta):
        return at(f, g - q + member(delta))

    barrier = pltpu.get_barrier_semaphore()

    def signal(sem, device):
        pl.semaphore_signal(sem, inc=1, device_id=device, device_id_type=MESH)

    for k in OTHERS:
        signal(barrier, at(z * 8 + y_peer(k) * 2, g))

    @pl.when(c == 1)
    def _():
        signal(barrier, core_dev)

    signal(barrier, at((1 - z) * 8 + y * 2 + 1, g))
    for delta in range(1, GROUP):
        signal(barrier, at(z * 8 + y * 2 + 1, g - q + member(delta)))

    def near_ready():
        @pl.when(c == 0)
        def _():
            pl.semaphore_wait(barrier, 2 * YS - 1)
            signal(near_sem, core_dev)

        @pl.when(c == 1)
        def _():
            pl.semaphore_wait(near_sem, 1)

    def far_ready():
        @pl.when(c == 1)
        def _():
            pl.semaphore_wait(barrier, 2 * GROUP)
            signal(far_sem, core_dev)

        @pl.when(c == 0)
        def _():
            pl.semaphore_wait(far_sem, 1)

    count = [0, 0]
    stage = [0]
    bytes_sent = [0] * (STEPS + 1)

    named = {}

    def new_group(*name):
        if name and name in named:
            return named[name]
        count[0] += 1
        named[name] = count[0] - 1
        return count[0] - 1

    def remote(src, dst, device, group):
        pltpu.make_async_remote_copy(
            src_ref=src, dst_ref=dst, send_sem=send_sem.at[stage[0]], recv_sem=recv_sem.at[group],
            device_id=device, device_id_type=MESH,
        ).start()
        rows = math.prod(src.shape) // RANK
        bytes_sent[stage[0]] += rows

    def arrive(group, like):
        pltpu.make_async_remote_copy(
            src_ref=like, dst_ref=like, send_sem=send_sem.at[0], recv_sem=recv_sem.at[group],
            device_id=core_dev, device_id_type=MESH,
        ).wait_recv()

    def flush(which):
        like = bulk.at[pl.ds(0, bytes_sent[which]), :]
        pltpu.make_async_remote_copy(
            src_ref=like, dst_ref=like, send_sem=send_sem.at[which], recv_sem=recv_sem.at[0],
            device_id=core_dev, device_id_type=MESH,
        ).wait_send()
        bytes_sent[which] = 0

    def loaded(copy):
        copy.wait()

    def local(src, dst):
        i = count[1]
        count[1] += 1
        copy = pltpu.make_async_copy(src, dst, local_sem.at[i])
        copy.start()
        return copy

    def feature_cols(p, who):
        return pl.ds(pl.multiple_of(p * HALF + who * CHIP_ROWS, 128), CHIP_ROWS)

    def doc_rows(who):
        return pl.ds(pl.multiple_of(who * DOC, DOC), DOC)

    def rows_of(core):
        return pl.ds(pl.multiple_of(core * ROWS, 64), ROWS)

    def cols(h):
        return slice(h * RANK, (h + 1) * RANK)

    my_half = pl.ds(pl.multiple_of(c * (RANK // 2), RANK // 2), RANK // 2)
    other_half = pl.ds(pl.multiple_of((1 - c) * (RANK // 2), RANK // 2), RANK // 2)

    def dot(a, b):
        return jnp.dot(a, b, preferred_element_type=F32)

    def tdot(a, b):
        return lax.dot_general(a, b, (((0,), (0,)), ((), ())), preferred_element_type=F32)

    def send_tokens(s):
        groups = {k: new_group("tok", k) for k in OTHERS}
        for k, p in ((1, 0), (3, 0), (1, 1), (3, 1), (2, 0), (2, 1)):
            remote(docs.at[s, :, feature_cols(p, y_peer(k))], xs.at[s, p, doc_rows(y), :], y_dev(k), groups[k])
        return groups

    def send_weights(s, h):
        own = wire.at[s, h, z, rows_of(c), :]
        groups = new_group("wz", h), new_group("wc", h)
        remote(own, own, z_dev, groups[0])
        remote(own, own, core_dev, groups[1])
        return groups

    def forward_weights(s, h):
        got = wire.at[s, h, 1 - z, rows_of(c), :]
        group = new_group("wf", h)
        arrive(w_groups[h][0], got)
        remote(got, got, core_dev, group)
        return group

    def weights_here(group, s, h, p):
        arrive(group, wire.at[s, h, p, rows_of(1 - c), :])

    in_weight = local(master.at[0], weight)
    in_doc = [local(tokens.at[0, 0], docs.at[0])]
    loaded(in_weight)
    for h in (0, 1):
        wire[0, h, z, rows_of(c), :] = weight[:, cols(h)].astype(BF16)
    loaded(in_doc[0])
    near_ready()
    tok_groups = [send_tokens(0)]
    far_ready()
    w_groups = [send_weights(0, h) for h in (0, 1)]
    in_doc.append(local(tokens.at[1, 0], docs.at[1]))
    in_own = [
        [local(tokens.at[s, 0, :, feature_cols(p, y)], xs.at[s, p, doc_rows(y), :]) for p in (0, 1)]
        for s in range(STEPS)
    ]
    in_first = local(moment.at[0], first)
    in_squares = local(second.at[0], squares)

    m = D**-0.5
    r = RANK**-0.5
    alpha = (RANK / GROUP_TOK) ** 0.5
    tall = (DOC, RANK)

    def gram_of(s):
        x = docs[s]
        xgram[s] = lax.dot_general(x, x, (((1,), (1,)), ((), ())), preferred_element_type=F32)

    gram_of(0)

    for s in range(STEPS):

        def part_product(who, h, p):
            return dot(xs[s, p, doc_rows(who), :], wire[s, h, p])

        def part_gram(p, core):
            right[...] = wire[s, 1, p, rows_of(core), :]
            return tdot(right[...], right[...])

        def tokens_here(k):
            arrive(tok_groups[s][k], xs.at[s, :, doc_rows((y + YS - k) % YS), :])

        gram_group, p_groups = new_group("gram"), (new_group("p", 0), new_group("p", 1))

        def send_gram(gram):
            gram_send[s] = gram.astype(BF16)
            for k in OTHERS:
                remote(gram_send.at[s], gram_recv.at[s, k - 1], y_dev(k), gram_group)

        def gram_sum(gram):
            arrive(gram_group, gram_recv.at[s])
            for k in range(3):
                gram += gram_recv[s, k].astype(F32)
            return gram

        def send_product(k, h, value):
            psend[s, h, k - 1] = value.astype(BF16)
            remote(psend.at[s, h, k - 1], prec.at[s, h, k - 1], y_dev(k), p_groups[h])

        if s == 0:
            forwards = [forward_weights(s, h) for h in (0, 1)]
            for h in (0, 1):
                weights_here(w_groups[h][1], s, h, z)
                weights_here(forwards[h], s, h, 1 - z)
            gram_full[...] = sum(part_gram(p, core) for p in (0, 1) for core in (0, 1))
            core_gram_send[0] = gram_full[my_half, :].astype(BF16)
            for k in OTHERS:
                remote(core_gram_send.at[0], core_gram_recv.at[k - 1], y_dev(k), gram_group)
            for copy in in_own[s]:
                loaded(copy)
            for p in (0, 1):
                wide[p] = jnp.concatenate([wire[s, 0, p], wire[s, 1, p]], axis=1)

            def whole_product(who):
                return sum(dot(xs[s, p, doc_rows(who), :], wide[p]) for p in (0, 1))

            for k in OTHERS:
                tokens_here(YS - k)
                value = whole_product(y_peer(k))
                for h in (0, 1):
                    send_product(k, h, value[:, cols(h)])
            arrive(gram_group, core_gram_recv.at[pl.ds(0, 3)])
            half_sum = gram_full[my_half, :] + sum(core_gram_recv[k].astype(F32) for k in range(3))
            core_gram_send[1] = half_sum.astype(BF16)
            half_group = new_group()
            remote(core_gram_send.at[1], core_gram_recv.at[3], core_dev, half_group)
            gram_full[my_half, :] = half_sum
            value = whole_product(y)
            for h in (0, 1):
                pacc[h, 0] = value[:, cols(h)]
        else:
            weights_here(w_groups[1][1], s, 1, z)
            gram = part_gram(z, c) + part_gram(z, 1 - c)
            send_gram(gram)
            weights_here(w_groups[0][1], s, 0, z)
            for copy in in_own[s]:
                loaded(copy)
            for k in OTHERS:
                tokens_here(k)
            for k in range(YS):
                pacc[0, k] = part_product(y_peer(k), 0, z)
                pacc[1, k] = part_product(y_peer(k), 1, z)
            forward = forward_weights(s, 0)
            gram = gram_sum(gram)
            half_send[...] = gram.astype(BF16)
            half_group = new_group()
            remote(half_send, half_recv, z_dev, half_group)
            weights_here(forward, s, 0, 1 - z)
            for k in OTHERS:
                send_product(k, 0, pacc[0, k] + part_product(y_peer(k), 0, 1 - z))
            pacc[0, 0] += part_product(y, 0, 1 - z)
            forward = forward_weights(s, 1)
            weights_here(forward, s, 1, 1 - z)
            for k in OTHERS:
                send_product(k, 1, pacc[1, k] + part_product(y_peer(k), 1, 1 - z))
            pacc[1, 0] += part_product(y, 1, 1 - z)

        for p in (0, 1):
            xt[p] = xs[s, p].T
        at_t = lax.broadcasted_iota(jnp.int32, tall, 0)
        at_j = lax.broadcasted_iota(jnp.int32, tall, 1)
        xx = xgram[s]
        sx = jnp.sum(jnp.where(at_j == at_t, xx, 0.0), axis=1, keepdims=True)
        xn = jnp.sum(jnp.where(at_j == at_t + 1, xx, 0.0), axis=1, keepdims=True)
        ix = lax.rsqrt(sx * (1.0 / D) + 1e-5)
        ixn = pltpu.roll(jnp.broadcast_to(ix, tall), DOC - 1, 0)[:, :1]
        kept = jnp.where(lax.broadcasted_iota(jnp.int32, (DOC, 1), 0) == DOC - 1, 0.0, alpha)

        if s == 0:
            arrive(half_group, core_gram_recv.at[3])
            gram_full[other_half, :] = core_gram_recv[3].astype(F32)
            gram = gram_full[...]
        else:
            arrive(half_group, half_recv)
            gram += half_recv[...].astype(F32)
        ghi = gram.astype(BF16)
        glo = (gram - ghi.astype(F32)).astype(BF16)
        arrive(p_groups[0], prec.at[s, 0])
        left = pacc[0, 0]
        for k in range(3):
            left += prec[s, 0, k].astype(F32)
        low = (ix * left * m).astype(BF16)
        lowf = low.astype(F32)
        lowg = dot(low, ghi) + dot(low, glo)
        arrive(p_groups[1], prec.at[s, 1])
        pr = pacc[1, 0]
        for k in range(3):
            pr += prec[s, 1, k].astype(F32)

        prn = pltpu.roll(pr, DOC - 1, 0)
        oo = (
            sx
            + (2 * r) * jnp.sum(lowf * pr, axis=1, keepdims=True)
            + (r * r) * jnp.sum(lowf * lowg, axis=1, keepdims=True)
        )
        inv = lax.rsqrt(oo * (1.0 / D) + 1e-5)
        sno = ixn * (xn + r * jnp.sum(lowf * prn, axis=1, keepdims=True))
        cc = kept * (inv * inv * oo - inv * sno) * (1.0 / D)
        aa = inv * inv * (kept - cc)
        bb = kept * inv * ixn
        dlow = (aa * (pr + r * lowg) - bb * prn) * (RANK * D) ** -0.5
        e_groups = []

        def send_factor(kind, value):
            eall[s, kind, y] = value.astype(BF16)
            e_groups.append(new_group("e", kind))
            for k in OTHERS:
                remote(eall.at[s, kind, y], eall.at[s, kind, y], y_dev(k), e_groups[kind])

        send_factor(0, ix * dlow)
        al = aa * lowf
        send_factor(1, r * (al - pltpu.roll(bb * lowf, 1, 0)))
        send_factor(2, (r * r) * tdot(low, al.astype(BF16)))
        if s + 1 < STEPS:
            stage[0] = s + 1
            loaded(in_doc[s + 1])
            tok_groups.append(send_tokens(s + 1))
        own_groups = []
        z_groups = []
        for h in (0, 1):
            for kind in (0,) if h == 0 else (1, 2):
                arrive(e_groups[kind], eall.at[s, kind, pl.ds(0, YS - 1)])
            factor = eall[s, h].reshape(YS * DOC, RANK)
            if h == 1:
                outer = sum(eall[s, 2, j].astype(F32) for j in range(YS)).astype(BF16)

            def gradient(p, core):
                rows = dot(xt[p, rows_of(core), :], factor)
                if h == 1:
                    rows += dot(wire[s, 1, p, rows_of(core), :], outer)
                return rows

            dsend[s, h, 0] = gradient(1 - z, 1 - c).astype(BF16)
            cross = new_group("cross", h)
            remote(dsend.at[s, h, 0], drec.at[s, h, 0], core_dev, cross)
            keep_cross[...] = gradient(1 - z, c)
            dsend[s, h, 1] = gradient(z, 1 - c).astype(BF16)
            own_groups.append(new_group("own", h))
            remote(dsend.at[s, h, 1], drec.at[s, h, 1], core_dev, own_groups[h])
            arrive(cross, drec.at[s, h, 0])
            zsend[s, h] = (keep_cross[...] + drec[s, h, 0].astype(F32)).astype(BF16)
            z_groups.append(new_group("z", h))
            remote(zsend.at[s, h], zrec.at[s, h], z_dev, z_groups[h])
            keep_own[h] = gradient(z, c)
        if s == 0:
            loaded(in_first)
            loaded(in_squares)
            gram_of(1)
        for h in (0, 1):
            arrive(own_groups[h], drec.at[s, h, 1])
            keep_own[h] += drec[s, h, 1].astype(F32)
        w_groups = []
        g_groups = []
        if s + 1 == STEPS:
            stage[0] = STEPS
        for h in (0, 1):
            arrive(z_groups[h], zrec.at[s, h])
            grad = keep_own[h] + zrec[s, h].astype(F32)
            one = 0.9 * first[:, cols(h)] + 0.1 * grad
            two = 0.95 * squares[:, cols(h)] + 0.05 * grad * grad
            new = weight[:, cols(h)] - 0.02 * one / (jnp.sqrt(two) + 1e-8)
            first[:, cols(h)] = one
            squares[:, cols(h)] = two
            weight[:, cols(h)] = new
            wire[s + 1, h, z, rows_of(c), :] = new.astype(BF16)
            if s + 1 < STEPS:
                w_groups.append(send_weights(s + 1, h))
                continue
            g_groups.append(new_group())
            for delta in range(1, GROUP):
                start = c * ROWS + part_start(member(delta))
                rows = pl.ds(pl.multiple_of(start, 16), PART)
                remote(wire.at[STEPS, h, z, rows, :], grec.at[h, delta - 1], gossip_dev(delta), g_groups[h])

    outs = [local(first, mom_out.at[0]), local(squares, sec_out.at[0])]
    share = []
    for b in range(3):
        used = sum((cube[i] == b).astype(jnp.int32) for i in range(4))
        share.append(0.5 * jnp.minimum(used, 1).astype(F32))
    a_groups = []
    for h in (0, 1):
        held = [weight[pl.ds(part_start(q), PART), cols(h)]]
        arrive(g_groups[h], grec.at[h])
        for delta in range(1, GROUP):
            held.append(grec[h, delta - 1].astype(F32))
        for b in range(3):
            held = [held[d] + share[b] * (held[d ^ (1 << b)] - held[d]) for d in range(GROUP)]
        a_groups.append(new_group())
        for delta in range(1, GROUP):
            gsend[h, delta - 1] = held[delta].astype(BF16)
            remote(gsend.at[h, delta - 1], arec.at[h, delta - 1], gossip_dev(delta), a_groups[h])
        averaged[h, pl.ds(part_start(q), PART), :] = held[0]
    for which in range(STEPS):
        flush(which)
    for h in (0, 1):
        arrive(a_groups[h], arec.at[h])
        for delta in range(1, GROUP):
            averaged[h, pl.ds(part_start(member(delta)), PART), :] = arec[h, delta - 1].astype(F32)
        outs.append(local(averaged.at[h], avg_out.at[0, :, cols(h)]))

    flush(STEPS)
    for copy in outs:
        loaded(copy)


def store_kernel(*refs):
    ins, outs, held, sems = refs[:3], refs[3:6], refs[6:9], refs[9]
    reads = [pltpu.make_async_copy(ins[i], held[i], sems.at[i]) for i in range(3)]
    writes = [pltpu.make_async_copy(held[i], outs[i], sems.at[3 + i]) for i in range(3)]
    for copy in reads:
        copy.start()
    for i in range(3):
        reads[i].wait()
        writes[i].start()
    for copy in writes:
        copy.wait()


def body(tokens, master, moment, second, cube_bit):
    any_space = pl.BlockSpec(memory_space=pl.ANY)
    rows = jax.ShapeDtypeStruct((1, ROWS, 2 * RANK), F32)
    scratch = [
        pltpu.VMEM((ROWS, 2 * RANK), F32),
        pltpu.VMEM((ROWS, 2 * RANK), F32),
        pltpu.VMEM((ROWS, 2 * RANK), F32),
        pltpu.VMEM((STEPS + 1, 2, 2, CHIP_ROWS, RANK), BF16),
        pltpu.VMEM((STEPS, DOC, D), BF16),
        pltpu.VMEM((STEPS, 2, YS * DOC, CHIP_ROWS), BF16),
        pltpu.VMEM((2, CHIP_ROWS, YS * DOC), BF16),
        pltpu.VMEM((STEPS, DOC, DOC), F32),
        pltpu.VMEM((2, YS, DOC, RANK), F32),
        pltpu.VMEM((2, CHIP_ROWS, 2 * RANK), BF16),
        pltpu.VMEM((STEPS, RANK, RANK), BF16),
        pltpu.VMEM((STEPS, 3, RANK, RANK), BF16),
        pltpu.VMEM((RANK, RANK), BF16),
        pltpu.VMEM((RANK, RANK), BF16),
        pltpu.VMEM((RANK, RANK), F32),
        pltpu.VMEM((2, RANK // 2, RANK), BF16),
        pltpu.VMEM((4, RANK // 2, RANK), BF16),
        pltpu.VMEM((STEPS, 2, 3, DOC, RANK), BF16),
        pltpu.VMEM((STEPS, 2, 3, DOC, RANK), BF16),
        pltpu.VMEM((STEPS, 3, YS, DOC, RANK), BF16),
        pltpu.VMEM((ROWS, RANK), BF16),
        pltpu.VMEM((ROWS, RANK), F32),
        pltpu.VMEM((2, ROWS, RANK), F32),
        pltpu.VMEM((STEPS, 2, 2, ROWS, RANK), BF16),
        pltpu.VMEM((STEPS, 2, 2, ROWS, RANK), BF16),
        pltpu.VMEM((STEPS, 2, ROWS, RANK), BF16),
        pltpu.VMEM((STEPS, 2, ROWS, RANK), BF16),
        pltpu.VMEM((2, GROUP - 1, PART, RANK), BF16),
        pltpu.VMEM((2, GROUP - 1, PART, RANK), BF16),
        pltpu.VMEM((2, GROUP - 1, PART, RANK), BF16),
        pltpu.VMEM((2, ROWS, RANK), F32),
        pltpu.VMEM((BULK, RANK), BF16),
        pltpu.SemaphoreType.DMA((STEPS + 1,)),
        pltpu.SemaphoreType.DMA((N_GROUPS,)),
        pltpu.SemaphoreType.DMA((N_LOCAL,)),
        pltpu.SemaphoreType.REGULAR,
        pltpu.SemaphoreType.REGULAR,
    ]
    outs = pl.pallas_call(
        kernel,
        out_shape=(rows, rows, rows),
        in_specs=[any_space] * 4 + [pl.BlockSpec(memory_space=pltpu.SMEM)],
        out_specs=(any_space,) * 3,
        scratch_shapes=scratch,
        compiler_params=pltpu.CompilerParams(
            collective_id=0, has_side_effects=True, vmem_limit_bytes=VMEM_LIMIT
        ),
        name="train",
    )(tokens, master, moment, second, cube_bit)
    return pl.pallas_call(
        store_kernel,
        out_shape=(rows, rows, rows),
        in_specs=[any_space] * 3,
        out_specs=(any_space,) * 3,
        scratch_shapes=[pltpu.VMEM((1, ROWS, 2 * RANK), F32)] * 3 + [pltpu.SemaphoreType.DMA((6,))],
        compiler_params=pltpu.CompilerParams(vmem_limit_bytes=VMEM_LIMIT),
        name="store",
    )(*outs)


def solution(mesh):
    in_specs = (
        P(None, "gossip", "fsdp", None),
        P("gossip", "fsdp", None),
        P("gossip", "fsdp", None),
        P("gossip", "fsdp", None),
        P(),
    )
    out_specs = (P("gossip", "fsdp", None), P("gossip", "fsdp", None), P("gossip", "fsdp", None))
    return jax.shard_map(body, mesh=mesh, in_specs=in_specs, out_specs=out_specs, check_vma=False)
```

```python
import math

import jax
import jax.numpy as jnp
from jax import lax
from jax.experimental import pallas as pl
from jax.experimental.pallas import tpu as pltpu
from jax.sharding import PartitionSpec as P

MESH = pl.DeviceIdType.MESH
F32, BF16 = jnp.float32, jnp.bfloat16

D = 5120
RANK = 128
STEPS = 2
DOC = 128
GROUP_TOK = 2048
ROWS = 320
CHIP_ROWS = 640
HALF = 2560
YS = 4
GROUP = 8
PART = 48
N_GROUPS = 27
N_LOCAL = 13
BULK = 12288
VMEM_LIMIT = 60 * 1024 * 1024
OTHERS = (1, 3, 2)


def part_start(member):
    return pl.multiple_of(16 * ((5 * member) // 2), 16)


def kernel(
    tokens, master, moment, second, cube, avg_out, mom_out, sec_out,
    weight, first, squares, wire, docs, xs, xt, xgram, pacc, wide, gram_send, gram_recv, half_send, half_recv,
    gram_full, core_gram_send, core_gram_recv, psend, prec, eall, right,
    keep_cross, keep_own, dsend, drec, zsend, zrec, grec, gsend, arec, averaged,
    bulk, send_sem, recv_sem, local_sem, near_sem, far_sem,
):
    f = lax.axis_index("fsdp")
    g = lax.axis_index("gossip")
    z, y, c = f // 8, (f // 2) % YS, f % 2
    q = g % GROUP

    def at(fi, gi):
        return {"fsdp": fi, "gossip": gi}

    def y_peer(k):
        return (y + k) % YS

    def y_dev(k):
        return at(z * 8 + y_peer(k) * 2 + c, g)

    core_dev = at(z * 8 + y * 2 + (1 - c), g)
    z_dev = at((1 - z) * 8 + y * 2 + c, g)

    def member(delta):
        bits = [(q // (1 << b)) % 2 for b in range(3)]
        return sum((1 - bits[b] if (delta >> b) & 1 else bits[b]) * (1 << b) for b in range(3))

    def gossip_dev(delta):
        return at(f, g - q + member(delta))

    barrier = pltpu.get_barrier_semaphore()

    def signal(sem, device):
        pl.semaphore_signal(sem, inc=1, device_id=device, device_id_type=MESH)

    for k in OTHERS:
        signal(barrier, at(z * 8 + y_peer(k) * 2, g))

    @pl.when(c == 1)
    def _():
        signal(barrier, core_dev)

    signal(barrier, at((1 - z) * 8 + y * 2 + 1, g))
    for delta in range(1, GROUP):
        signal(barrier, at(z * 8 + y * 2 + 1, g - q + member(delta)))

    def near_ready():
        @pl.when(c == 0)
        def _():
            pl.semaphore_wait(barrier, 2 * YS - 1)
            signal(near_sem, core_dev)

        @pl.when(c == 1)
        def _():
            pl.semaphore_wait(near_sem, 1)

    def far_ready():
        @pl.when(c == 1)
        def _():
            pl.semaphore_wait(barrier, 2 * GROUP)
            signal(far_sem, core_dev)

        @pl.when(c == 0)
        def _():
            pl.semaphore_wait(far_sem, 1)

    count = [0, 0]
    stage = [0]
    bytes_sent = [0] * (STEPS + 1)

    named = {}

    def new_group(*name):
        if name and name in named:
            return named[name]
        count[0] += 1
        named[name] = count[0] - 1
        return count[0] - 1

    def remote(src, dst, device, group):
        pltpu.make_async_remote_copy(
            src_ref=src, dst_ref=dst, send_sem=send_sem.at[stage[0]], recv_sem=recv_sem.at[group],
            device_id=device, device_id_type=MESH,
        ).start()
        rows = math.prod(src.shape) // RANK
        bytes_sent[stage[0]] += rows

    def arrive(group, like):
        pltpu.make_async_remote_copy(
            src_ref=like, dst_ref=like, send_sem=send_sem.at[0], recv_sem=recv_sem.at[group],
            device_id=core_dev, device_id_type=MESH,
        ).wait_recv()

    def flush(which):
        like = bulk.at[pl.ds(0, bytes_sent[which]), :]
        pltpu.make_async_remote_copy(
            src_ref=like, dst_ref=like, send_sem=send_sem.at[which], recv_sem=recv_sem.at[0],
            device_id=core_dev, device_id_type=MESH,
        ).wait_send()
        bytes_sent[which] = 0

    def loaded(copy):
        copy.wait()

    def local(src, dst):
        i = count[1]
        count[1] += 1
        copy = pltpu.make_async_copy(src, dst, local_sem.at[i])
        copy.start()
        return copy

    def feature_cols(p, who):
        return pl.ds(pl.multiple_of(p * HALF + who * CHIP_ROWS, 128), CHIP_ROWS)

    def doc_rows(who):
        return pl.ds(pl.multiple_of(who * DOC, DOC), DOC)

    def rows_of(core):
        return pl.ds(pl.multiple_of(core * ROWS, 64), ROWS)

    def cols(h):
        return slice(h * RANK, (h + 1) * RANK)

    my_half = pl.ds(pl.multiple_of(c * (RANK // 2), RANK // 2), RANK // 2)
    other_half = pl.ds(pl.multiple_of((1 - c) * (RANK // 2), RANK // 2), RANK // 2)

    def dot(a, b):
        return jnp.dot(a, b, preferred_element_type=F32)

    def tdot(a, b):
        return lax.dot_general(a, b, (((0,), (0,)), ((), ())), preferred_element_type=F32)

    def send_tokens(s):
        groups = {k: new_group("tok", k) for k in OTHERS}
        for k, p in ((1, 0), (3, 0), (1, 1), (3, 1), (2, 0), (2, 1)):
            remote(docs.at[s, :, feature_cols(p, y_peer(k))], xs.at[s, p, doc_rows(y), :], y_dev(k), groups[k])
        return groups

    def send_weights(s, h):
        own = wire.at[s, h, z, rows_of(c), :]
        groups = new_group("wz", h), new_group("wc", h)
        remote(own, own, z_dev, groups[0])
        remote(own, own, core_dev, groups[1])
        return groups

    def forward_weights(s, h):
        got = wire.at[s, h, 1 - z, rows_of(c), :]
        group = new_group("wf", h)
        arrive(w_groups[h][0], got)
        remote(got, got, core_dev, group)
        return group

    def weights_here(group, s, h, p):
        arrive(group, wire.at[s, h, p, rows_of(1 - c), :])

    in_weight = local(master.at[0], weight)
    in_doc = [local(tokens.at[0, 0], docs.at[0])]
    loaded(in_weight)
    for h in (0, 1):
        wire[0, h, z, rows_of(c), :] = weight[:, cols(h)].astype(BF16)
    loaded(in_doc[0])
    near_ready()
    tok_groups = [send_tokens(0)]
    far_ready()
    w_groups = [send_weights(0, h) for h in (0, 1)]
    in_doc.append(local(tokens.at[1, 0], docs.at[1]))
    in_own = [
        [local(tokens.at[s, 0, :, feature_cols(p, y)], xs.at[s, p, doc_rows(y), :]) for p in (0, 1)]
        for s in range(STEPS)
    ]
    in_first = local(moment.at[0], first)
    in_squares = local(second.at[0], squares)

    m = D**-0.5
    r = RANK**-0.5
    alpha = (RANK / GROUP_TOK) ** 0.5
    tall = (DOC, RANK)

    def gram_of(s):
        x = docs[s]
        xgram[s] = lax.dot_general(x, x, (((1,), (1,)), ((), ())), preferred_element_type=F32)

    gram_of(0)

    for s in range(STEPS):

        def part_product(who, h, p):
            return dot(xs[s, p, doc_rows(who), :], wire[s, h, p])

        def part_gram(p, core):
            right[...] = wire[s, 1, p, rows_of(core), :]
            return tdot(right[...], right[...])

        def tokens_here(k):
            arrive(tok_groups[s][k], xs.at[s, :, doc_rows((y + YS - k) % YS), :])

        gram_group, p_groups = new_group("gram"), (new_group("p", 0), new_group("p", 1))

        def send_gram(gram):
            gram_send[s] = gram.astype(BF16)
            for k in OTHERS:
                remote(gram_send.at[s], gram_recv.at[s, k - 1], y_dev(k), gram_group)

        def gram_sum(gram):
            arrive(gram_group, gram_recv.at[s])
            for k in range(3):
                gram += gram_recv[s, k].astype(F32)
            return gram

        def send_product(k, h, value):
            psend[s, h, k - 1] = value.astype(BF16)
            remote(psend.at[s, h, k - 1], prec.at[s, h, k - 1], y_dev(k), p_groups[h])

        if s == 0:
            forwards = [forward_weights(s, h) for h in (0, 1)]
            for h in (0, 1):
                weights_here(w_groups[h][1], s, h, z)
                weights_here(forwards[h], s, h, 1 - z)
            gram_full[...] = sum(part_gram(p, core) for p in (0, 1) for core in (0, 1))
            core_gram_send[0] = gram_full[my_half, :].astype(BF16)
            for k in OTHERS:
                remote(core_gram_send.at[0], core_gram_recv.at[k - 1], y_dev(k), gram_group)
            for copy in in_own[s]:
                loaded(copy)
            for p in (0, 1):
                wide[p] = jnp.concatenate([wire[s, 0, p], wire[s, 1, p]], axis=1)

            def whole_product(who):
                return sum(dot(xs[s, p, doc_rows(who), :], wide[p]) for p in (0, 1))

            for k in OTHERS:
                tokens_here(YS - k)
                value = whole_product(y_peer(k))
                for h in (0, 1):
                    send_product(k, h, value[:, cols(h)])
            arrive(gram_group, core_gram_recv.at[pl.ds(0, 3)])
            half_sum = gram_full[my_half, :] + sum(core_gram_recv[k].astype(F32) for k in range(3))
            core_gram_send[1] = half_sum.astype(BF16)
            half_group = new_group()
            remote(core_gram_send.at[1], core_gram_recv.at[3], core_dev, half_group)
            gram_full[my_half, :] = half_sum
            value = whole_product(y)
            for h in (0, 1):
                pacc[h, 0] = value[:, cols(h)]
        else:
            weights_here(w_groups[1][1], s, 1, z)
            gram = part_gram(z, c) + part_gram(z, 1 - c)
            send_gram(gram)
            weights_here(w_groups[0][1], s, 0, z)
            for copy in in_own[s]:
                loaded(copy)
            for k in OTHERS:
                tokens_here(k)
            for k in range(YS):
                pacc[0, k] = part_product(y_peer(k), 0, z)
                pacc[1, k] = part_product(y_peer(k), 1, z)
            forward = forward_weights(s, 0)
            gram = gram_sum(gram)
            half_send[...] = gram.astype(BF16)
            half_group = new_group()
            remote(half_send, half_recv, z_dev, half_group)
            weights_here(forward, s, 0, 1 - z)
            for k in OTHERS:
                send_product(k, 0, pacc[0, k] + part_product(y_peer(k), 0, 1 - z))
            pacc[0, 0] += part_product(y, 0, 1 - z)
            forward = forward_weights(s, 1)
            weights_here(forward, s, 1, 1 - z)
            for k in OTHERS:
                send_product(k, 1, pacc[1, k] + part_product(y_peer(k), 1, 1 - z))
            pacc[1, 0] += part_product(y, 1, 1 - z)

        for p in (0, 1):
            xt[p, :, : YS * DOC] = xs[s, p].T
            xt[p, :, YS * DOC :] = wire[s, 1, p]
        at_t = lax.broadcasted_iota(jnp.int32, tall, 0)
        at_j = lax.broadcasted_iota(jnp.int32, tall, 1)
        xx = xgram[s]
        sx = jnp.sum(jnp.where(at_j == at_t, xx, 0.0), axis=1, keepdims=True)
        xn = jnp.sum(jnp.where(at_j == at_t + 1, xx, 0.0), axis=1, keepdims=True)
        ix = lax.rsqrt(sx * (1.0 / D) + 1e-5)
        ixn = pltpu.roll(jnp.broadcast_to(ix, tall), DOC - 1, 0)[:, :1]
        kept = jnp.where(lax.broadcasted_iota(jnp.int32, (DOC, 1), 0) == DOC - 1, 0.0, alpha)

        if s == 0:
            arrive(half_group, core_gram_recv.at[3])
            gram_full[other_half, :] = core_gram_recv[3].astype(F32)
            gram = gram_full[...]
        else:
            arrive(half_group, half_recv)
            gram += half_recv[...].astype(F32)
        ghi = gram.astype(BF16)
        glo = (gram - ghi.astype(F32)).astype(BF16)
        arrive(p_groups[0], prec.at[s, 0])
        left = pacc[0, 0]
        for k in range(3):
            left += prec[s, 0, k].astype(F32)
        low = (ix * left * m).astype(BF16)
        lowf = low.astype(F32)
        lowg = dot(low, ghi) + dot(low, glo)
        arrive(p_groups[1], prec.at[s, 1])
        pr = pacc[1, 0]
        for k in range(3):
            pr += prec[s, 1, k].astype(F32)

        prn = pltpu.roll(pr, DOC - 1, 0)
        oo = (
            sx
            + (2 * r) * jnp.sum(lowf * pr, axis=1, keepdims=True)
            + (r * r) * jnp.sum(lowf * lowg, axis=1, keepdims=True)
        )
        inv = lax.rsqrt(oo * (1.0 / D) + 1e-5)
        sno = ixn * (xn + r * jnp.sum(lowf * prn, axis=1, keepdims=True))
        cc = kept * (inv * inv * oo - inv * sno) * (1.0 / D)
        aa = inv * inv * (kept - cc)
        bb = kept * inv * ixn
        dlow = (aa * (pr + r * lowg) - bb * prn) * (RANK * D) ** -0.5
        e_groups = []

        def send_factor(kind, value):
            eall[s, kind, y] = value.astype(BF16)
            e_groups.append(new_group("e", kind))
            for k in OTHERS:
                remote(eall.at[s, kind, y], eall.at[s, kind, y], y_dev(k), e_groups[kind])

        send_factor(0, ix * dlow)
        al = aa * lowf
        send_factor(1, r * (al - pltpu.roll(bb * lowf, 1, 0)))
        send_factor(2, (r * r) * tdot(low, al.astype(BF16)))
        if s + 1 < STEPS:
            stage[0] = s + 1
            loaded(in_doc[s + 1])
            tok_groups.append(send_tokens(s + 1))
        own_groups = []
        z_groups = []
        for h in (0, 1):
            for kind in (0,) if h == 0 else (1, 2):
                arrive(e_groups[kind], eall.at[s, kind, pl.ds(0, YS - 1)])
            factor = eall[s, h].reshape(YS * DOC, RANK)
            if h == 1:
                outer = sum(eall[s, 2, j].astype(F32) for j in range(YS)).astype(BF16)
                factor = jnp.concatenate([factor, outer], axis=0)

            def gradient(p, core):
                return dot(xt[p, rows_of(core), : factor.shape[0]], factor)

            dsend[s, h, 0] = gradient(1 - z, 1 - c).astype(BF16)
            cross = new_group("cross", h)
            remote(dsend.at[s, h, 0], drec.at[s, h, 0], core_dev, cross)
            keep_cross[...] = gradient(1 - z, c)
            dsend[s, h, 1] = gradient(z, 1 - c).astype(BF16)
            own_groups.append(new_group("own", h))
            remote(dsend.at[s, h, 1], drec.at[s, h, 1], core_dev, own_groups[h])
            arrive(cross, drec.at[s, h, 0])
            zsend[s, h] = (keep_cross[...] + drec[s, h, 0].astype(F32)).astype(BF16)
            z_groups.append(new_group("z", h))
            remote(zsend.at[s, h], zrec.at[s, h], z_dev, z_groups[h])
            keep_own[h] = gradient(z, c)
        if s == 0:
            loaded(in_first)
            loaded(in_squares)
            gram_of(1)
        for h in (0, 1):
            arrive(own_groups[h], drec.at[s, h, 1])
            keep_own[h] += drec[s, h, 1].astype(F32)
        w_groups = []
        g_groups = []
        if s + 1 == STEPS:
            stage[0] = STEPS
        for h in (0, 1):
            arrive(z_groups[h], zrec.at[s, h])
            grad = keep_own[h] + zrec[s, h].astype(F32)
            one = 0.9 * first[:, cols(h)] + 0.1 * grad
            two = 0.95 * squares[:, cols(h)] + 0.05 * grad * grad
            new = weight[:, cols(h)] - 0.02 * one / (jnp.sqrt(two) + 1e-8)
            first[:, cols(h)] = one
            squares[:, cols(h)] = two
            weight[:, cols(h)] = new
            wire[s + 1, h, z, rows_of(c), :] = new.astype(BF16)
            if s + 1 < STEPS:
                w_groups.append(send_weights(s + 1, h))
                continue
            g_groups.append(new_group())
            for delta in range(1, GROUP):
                start = c * ROWS + part_start(member(delta))
                rows = pl.ds(pl.multiple_of(start, 16), PART)
                remote(wire.at[STEPS, h, z, rows, :], grec.at[h, delta - 1], gossip_dev(delta), g_groups[h])

    outs = [local(first, mom_out.at[0]), local(squares, sec_out.at[0])]
    share = []
    for b in range(3):
        used = sum((cube[i] == b).astype(jnp.int32) for i in range(4))
        share.append(0.5 * jnp.minimum(used, 1).astype(F32))
    a_groups = []
    for h in (0, 1):
        held = [weight[pl.ds(part_start(q), PART), cols(h)]]
        arrive(g_groups[h], grec.at[h])
        for delta in range(1, GROUP):
            held.append(grec[h, delta - 1].astype(F32))
        for b in range(3):
            held = [held[d] + share[b] * (held[d ^ (1 << b)] - held[d]) for d in range(GROUP)]
        a_groups.append(new_group())
        for delta in range(1, GROUP):
            gsend[h, delta - 1] = held[delta].astype(BF16)
            remote(gsend.at[h, delta - 1], arec.at[h, delta - 1], gossip_dev(delta), a_groups[h])
        averaged[h, pl.ds(part_start(q), PART), :] = held[0]
    for which in range(STEPS):
        flush(which)
    for h in (0, 1):
        arrive(a_groups[h], arec.at[h])
        for delta in range(1, GROUP):
            averaged[h, pl.ds(part_start(member(delta)), PART), :] = arec[h, delta - 1].astype(F32)
        outs.append(local(averaged.at[h], avg_out.at[0, :, cols(h)]))

    flush(STEPS)
    for copy in outs:
        loaded(copy)


def store_kernel(*refs):
    ins, outs, held, sems = refs[:3], refs[3:6], refs[6:9], refs[9]
    reads = [pltpu.make_async_copy(ins[i], held[i], sems.at[i]) for i in range(3)]
    writes = [pltpu.make_async_copy(held[i], outs[i], sems.at[3 + i]) for i in range(3)]
    for copy in reads:
        copy.start()
    for i in range(3):
        reads[i].wait()
        writes[i].start()
    for copy in writes:
        copy.wait()


def body(tokens, master, moment, second, cube_bit):
    any_space = pl.BlockSpec(memory_space=pl.ANY)
    rows = jax.ShapeDtypeStruct((1, ROWS, 2 * RANK), F32)
    scratch = [
        pltpu.VMEM((ROWS, 2 * RANK), F32),
        pltpu.VMEM((ROWS, 2 * RANK), F32),
        pltpu.VMEM((ROWS, 2 * RANK), F32),
        pltpu.VMEM((STEPS + 1, 2, 2, CHIP_ROWS, RANK), BF16),
        pltpu.VMEM((STEPS, DOC, D), BF16),
        pltpu.VMEM((STEPS, 2, YS * DOC, CHIP_ROWS), BF16),
        pltpu.VMEM((2, CHIP_ROWS, YS * DOC + RANK), BF16),
        pltpu.VMEM((STEPS, DOC, DOC), F32),
        pltpu.VMEM((2, YS, DOC, RANK), F32),
        pltpu.VMEM((2, CHIP_ROWS, 2 * RANK), BF16),
        pltpu.VMEM((STEPS, RANK, RANK), BF16),
        pltpu.VMEM((STEPS, 3, RANK, RANK), BF16),
        pltpu.VMEM((RANK, RANK), BF16),
        pltpu.VMEM((RANK, RANK), BF16),
        pltpu.VMEM((RANK, RANK), F32),
        pltpu.VMEM((2, RANK // 2, RANK), BF16),
        pltpu.VMEM((4, RANK // 2, RANK), BF16),
        pltpu.VMEM((STEPS, 2, 3, DOC, RANK), BF16),
        pltpu.VMEM((STEPS, 2, 3, DOC, RANK), BF16),
        pltpu.VMEM((STEPS, 3, YS, DOC, RANK), BF16),
        pltpu.VMEM((ROWS, RANK), BF16),
        pltpu.VMEM((ROWS, RANK), F32),
        pltpu.VMEM((2, ROWS, RANK), F32),
        pltpu.VMEM((STEPS, 2, 2, ROWS, RANK), BF16),
        pltpu.VMEM((STEPS, 2, 2, ROWS, RANK), BF16),
        pltpu.VMEM((STEPS, 2, ROWS, RANK), BF16),
        pltpu.VMEM((STEPS, 2, ROWS, RANK), BF16),
        pltpu.VMEM((2, GROUP - 1, PART, RANK), BF16),
        pltpu.VMEM((2, GROUP - 1, PART, RANK), BF16),
        pltpu.VMEM((2, GROUP - 1, PART, RANK), BF16),
        pltpu.VMEM((2, ROWS, RANK), F32),
        pltpu.VMEM((BULK, RANK), BF16),
        pltpu.SemaphoreType.DMA((STEPS + 1,)),
        pltpu.SemaphoreType.DMA((N_GROUPS,)),
        pltpu.SemaphoreType.DMA((N_LOCAL,)),
        pltpu.SemaphoreType.REGULAR,
        pltpu.SemaphoreType.REGULAR,
    ]
    outs = pl.pallas_call(
        kernel,
        out_shape=(rows, rows, rows),
        in_specs=[any_space] * 4 + [pl.BlockSpec(memory_space=pltpu.SMEM)],
        out_specs=(any_space,) * 3,
        scratch_shapes=scratch,
        compiler_params=pltpu.CompilerParams(
            collective_id=0, has_side_effects=True, vmem_limit_bytes=VMEM_LIMIT
        ),
        name="train",
    )(tokens, master, moment, second, cube_bit)
    return pl.pallas_call(
        store_kernel,
        out_shape=(rows, rows, rows),
        in_specs=[any_space] * 3,
        out_specs=(any_space,) * 3,
        scratch_shapes=[pltpu.VMEM((1, ROWS, 2 * RANK), F32)] * 3 + [pltpu.SemaphoreType.DMA((6,))],
        compiler_params=pltpu.CompilerParams(vmem_limit_bytes=VMEM_LIMIT),
        name="store",
    )(*outs)


def solution(mesh):
    in_specs = (
        P(None, "gossip", "fsdp", None),
        P("gossip", "fsdp", None),
        P("gossip", "fsdp", None),
        P("gossip", "fsdp", None),
        P(),
    )
    out_specs = (P("gossip", "fsdp", None), P("gossip", "fsdp", None), P("gossip", "fsdp", None))
    return jax.shard_map(body, mesh=mesh, in_specs=in_specs, out_specs=out_specs, check_vma=False)
```
